32 devices in a mesh: seg: 2 (over x), blk: 16 (over z, y, core).
Axes of the slice: x: 2, y: 2, z: 4, core: 2. Of those that a mesh axis runs over, the one named last changes fastest.
Arguments:
- products: bfloat16 [2, 4096, 4096], P('seg', 'blk'), may hold values from -0.09375 to 0.09375
- compat: int32 [2, 16, 16], P('seg', 'blk'), may hold values 0 or 1
- sizes: int32 [2, 16], P('seg', 'blk'), may hold values from 1 to 256, 3072 in all within a row
Outputs:
- orthonormal: bfloat16 [2, 4096, 4096], P('seg', None, 'blk')
- accumulated: float32 [2, 16, 256, 256], P('seg', 'blk')
The draws below stay inside these ranges and needn't reach their ends.
Inputs may be any that keep to these rules, and one draw needn't show every extreme that they name: Each site's 16 sector sizes sum to 3072 and one of them is exactly 256.
All inputs are finite; a program needn't handle non-finite values. No bound on the sum of `compat` or of `sizes` on one device may be relied on, other than what follows from the above.
Results may differ from the reference program's by a relative error of at most 0.001.
Values may be sent and summed in bfloat16 or wider, within the bound.
No kernel may reach another device: no remote copies, remote signals or barrier semaphores. Data moves between devices by JAX's collectives and lax.ppermute only.
A program may use at most 64 MiB of HBM per device.

```python
import math
import jax
import jax.numpy as jnp
import numpy as np
from jax import lax

W = 16
B = 256
SECT = 16
SITES = 2


def with_ends(array, rng, smallest, high):
    longest = array.shape.index(max(array.shape))
    spots = []
    for shift in (0, 1):
        where = [jax.random.randint(jax.random.fold_in(rng, axis), (), 0, length) for axis, length in enumerate(array.shape)]
        where[longest] = (where[longest] + shift) % array.shape[longest]
        spots.append(tuple(where))
    return array.at[spots[0]].set(smallest).at[spots[1]].set(high)


def block_scale(own_key, extent, cuts, smallest, high):
    loudness = 1.0
    for axis_at, parts in cuts:
        draws = jax.random.uniform(jax.random.fold_in(jax.random.fold_in(own_key, 6), axis_at), (parts,), jnp.float32, smallest / len(cuts), high / len(cuts))
        loudness = loudness * jnp.repeat(jnp.exp(draws), extent[axis_at] // parts).reshape((-1,) + (1,) * (len(extent) - 1 - axis_at))
    return loudness


def profile(amount, total, most, slope):
    portions = [(1 << 20) // math.isqrt(grade ** slope) + 1 for grade in range(2, amount + 1)]
    surplus, counts = total - most - (amount - 1), [1] * (amount - 1)
    while surplus > 0:
        movable = [i for i in range(amount - 1) if counts[i] < most]
        pool, remaining = sum([portions[i] for i in movable]), surplus
        for i in movable:
            addition = min(most - counts[i], max(1, remaining * portions[i] // pool), surplus)
            counts[i] = counts[i] + addition
            surplus = surplus - addition
    return np.array([most] + counts)


def ragged(key, amount, total, limit, slope):
    if amount == 2:
        one = jax.random.randint(key, (), max(1, total - limit), min(limit, total - 1) + 1)
        return jnp.stack([one, total - one])
    sizes = jnp.asarray(profile(amount, total, limit, slope), jnp.int32)
    couples = (amount - 1) // 2
    giver, sink = sizes[1:1 + 2 * couples:2], sizes[2:2 + 2 * couples:2]
    margin = jnp.minimum(giver - 1, limit - sink)
    shifted = jax.random.randint(jax.random.fold_in(key, 1), (couples,), 0, 1 << 20) % (margin + 1)
    sizes = sizes.at[1:1 + 2 * couples:2].set(giver - shifted).at[2:2 + 2 * couples:2].set(sink + shifted)
    return sizes[jax.random.permutation(jax.random.fold_in(key, 2), amount)]


def gaussian(own_key, dims, spread, reach, cuts=(), kind=jnp.bfloat16):
    drawn = spread * jax.random.normal(own_key, dims, jnp.float32)
    if cuts:
        drawn = drawn * block_scale(own_key, dims, cuts, -0.22, 0.18)
    return jnp.clip(drawn, -reach, reach).astype(kind)


def setup_inputs(seed: int = 0) -> dict:
    arg_keys = jax.random.split(jax.random.key(seed), 4)
    return {
        "products": gaussian(arg_keys[0], (SITES, W * B, SECT * B), (W * B) ** -0.5, 0.09375, ((0, 2), (1, 16))),
        "compat": with_ends((jax.random.randint(arg_keys[1], (SITES, SECT, W), 0, 4) < 3).astype(jnp.int32), jax.random.fold_in(arg_keys[1], 1), 0, 1),
        "sizes": jax.vmap(lambda own: ragged(own, SECT, 3 * SECT * B // 4, B, 2))(jax.random.split(arg_keys[2], SITES)).reshape((SITES, SECT)).astype(jnp.int32),
    }


shift_value = 0.05

def factor_sector(panel_in, allowed, live_cols):
    total_rows = panel_in.shape[0]
    width_cols = panel_in.shape[1]
    gate_rows = jnp.repeat(allowed, total_rows // allowed.shape[0], total_repeat_length=total_rows).astype(jnp.bfloat16)
    masked = panel_in * gate_rows[:, None] * live_cols.astype(jnp.bfloat16)[None, :]
    gram_raw = jnp.dot(masked.T.astype(jnp.float32), masked.astype(jnp.float32), preferred_element_type=jnp.float32)
    identity = jnp.eye(width_cols, dtype=jnp.float32)
    lower_one = jnp.linalg.cholesky(gram_raw + shift_value * identity)
    first_t = jax.scipy.linalg.solve_triangular(lower_one, masked.astype(jnp.float32).T, lower=True)
    gram_two = jnp.dot(first_t, first_t.T, precision=lax.Precision.HIGHEST) + shift_value * identity
    lower_two = jnp.linalg.cholesky(gram_two)
    ortho_t = jax.scipy.linalg.solve_triangular(lower_two, first_t, lower=True)
    factor_r = jnp.dot(lower_two.T, lower_one.T, precision=lax.Precision.HIGHEST)
    return (ortho_t.T.astype(jnp.bfloat16), factor_r)

def reference(products, compat, sizes):
    columns = jnp.arange(B, dtype=jnp.int32)
    live = (columns[None, None, :] < sizes[:, :, None]).astype(jnp.int32)

    def per_sector(sector):
        start = (sector * B).astype(jnp.int32)
        panels = lax.dynamic_slice_in_dim(products, start, B, 2)
        allowed = lax.dynamic_index_in_dim(compat, sector, 1, keepdims=False)
        live_now = lax.dynamic_index_in_dim(live, sector, 1, keepdims=False)
        return jax.vmap(factor_sector)(panels, allowed, live_now)
    ortho_all, factor_all = lax.map(per_sector, jnp.arange(SECT, dtype=jnp.int32))
    orthonormal = ortho_all.transpose(1, 2, 0, 3).reshape(SITES, W * B, SECT * B)
    factor_sites = factor_all.transpose(1, 0, 2, 3)

    def advance(carry, factor_now):
        updated = jnp.einsum('kab,kbc->kac', factor_now, carry, precision=lax.Precision.HIGHEST)
        return (updated, updated)
    start_carry = jnp.broadcast_to(jnp.eye(B, dtype=jnp.float32), (SECT, B, B))
    _, accumulated = lax.scan(advance, start_carry, factor_sites)
    return (orthonormal, accumulated)
```

```python
import functools

import jax
import jax.numpy as jnp
from jax import lax
from jax.experimental import pallas as pl
from jax.experimental.pallas import tpu as pltpu
from jax.sharding import PartitionSpec as P

SHIFT = 0.05
HIGHEST = lax.Precision.HIGHEST
PARAMS = pltpu.CompilerParams(vmem_limit_bytes=48 << 20)
LANES = 128
SUB = 8


def wide(x, lanes):
    return jnp.concatenate([x] * (lanes // LANES), axis=1)


def split_columns(src, out, sems):
    count, _, width = out.shape
    copies = [
        pltpu.make_async_copy(src.at[0, :, pl.ds(k * width, width)], out.at[k], sems.at[k])
        for k in range(count)
    ]
    for copy in copies:
        copy.start()
    for copy in copies:
        copy.wait()


def factor_in_place(w, n, nb):
    row_at = lax.broadcasted_iota(jnp.int32, (SUB, LANES), 0)
    subs = nb // SUB
    for r0 in range(0, n, nb):
        p = [w[r0 + SUB * i : r0 + SUB * (i + 1), :] for i in range(subs)]
        for s in range(subs):
            cols = {}
            for i in range(s, subs):
                for c in range(SUB):
                    at = r0 + SUB * s + c
                    cols[i, c] = jnp.broadcast_to(p[i][:, at : at + 1], (SUB, LANES))
            pivots = jnp.ones((SUB, LANES), jnp.float32)
            for c in range(SUB):
                pivot = jnp.broadcast_to(cols[s, c][c : c + 1, :], (SUB, LANES))
                pivot = jnp.maximum(pivot, SHIFT * SHIFT)
                inverse = 1.0 / pivot
                pivots = jnp.where(row_at == c, pivot, pivots)
                row = jnp.broadcast_to(p[s][c : c + 1, :], p[s].shape)
                ahead = {
                    d: jnp.broadcast_to(cols[s, d][c : c + 1, :], (SUB, LANES)) for d in range(c + 1, SUB)
                }
                for i in range(s, subs):
                    times = cols[i, c] * inverse
                    if i == s:
                        if c == SUB - 1:
                            continue
                        times = jnp.where(row_at > c, times, 0.0)
                    p[i] = p[i] - wide(times, 2 * n) * row
                    for d in range(c + 1, SUB):
                        cols[i, d] = cols[i, d] - times * ahead[d]
            p[s] = p[s] * wide(lax.rsqrt(pivots), 2 * n)
        u = jnp.concatenate(p, axis=0)
        w[r0 : r0 + nb, :] = u
        end = r0 + nb
        if end < n:
            first = end // LANES * LANES
            last = n + -(-end // LANES) * LANES
            t = lax.dot_general(
                u[:, first:n],
                u[:, first:last],
                (((0,), (0,)), ((), ())),
                precision=HIGHEST,
                preferred_element_type=jnp.float32,
            )
            w[end:n, first:last] = w[end:n, first:last] - t[end - first :, :]


def gram_factor(nb, compat, size, panel, r_out, high_out, low_out, w):
    rows, n = panel.shape
    groups = compat.shape[1]
    each = rows // groups
    g = jnp.zeros((n, n), jnp.float32)
    for k in range(groups):
        block = panel[k * each : (k + 1) * each, :]
        part = lax.dot_general(block, block, (((0,), (0,)), ((), ())), preferred_element_type=jnp.float32)
        g = g + part * compat[0, k].astype(jnp.float32)
    i = lax.broadcasted_iota(jnp.int32, (n, n), 0)
    j = lax.broadcasted_iota(jnp.int32, (n, n), 1)
    live = jnp.logical_and(i < size[0, 0], j < size[0, 0])
    eye = (i == j).astype(jnp.float32)
    w[:, :n] = jnp.where(live, (1.0 + SHIFT) * g, 0.0) + (SHIFT * SHIFT) * eye
    w[:, n:] = eye
    factor_in_place(w, n, nb)
    r_out[...] = jnp.where(i <= j, w[:, :n], 0.0)
    inverse = jnp.where(jnp.logical_and(i >= j, live), w[:, n:], 0.0)
    high = inverse.astype(jnp.bfloat16)
    high_out[...] = high
    low_out[...] = (inverse - high.astype(jnp.float32)).astype(jnp.bfloat16)


def orthonormal_rows(compat, panel, high, low, out):
    k = pl.program_id(0)
    dims = (((1,), (1,)), ((), ()))
    block = panel[...]
    q = lax.dot_general(block, high[...], dims, preferred_element_type=jnp.float32)
    q = q + lax.dot_general(block, low[...], dims, preferred_element_type=jnp.float32)
    out[0] = (q * compat[0, k].astype(jnp.float32)).astype(jnp.bfloat16)


def chained(by, own, incoming, out):
    later = lax.axis_index("seg") >= by

    @pl.when(later)
    def _():
        out[...] = jnp.dot(own[...], incoming[...], precision=HIGHEST, preferred_element_type=jnp.float32)

    @pl.when(jnp.logical_not(later))
    def _():
        out[...] = own[...]


def local(products, compat, sizes):
    parts = lax.axis_size("blk")
    rows_here, width = products.shape[1], products.shape[2] // parts
    rows = rows_here * parts
    groups = compat.shape[2]
    f32 = functools.partial(jax.ShapeDtypeStruct, dtype=jnp.float32)
    b16 = functools.partial(jax.ShapeDtypeStruct, dtype=jnp.bfloat16)
    in_smem = pl.BlockSpec(memory_space=pltpu.SMEM)
    in_vmem = pl.BlockSpec(memory_space=pltpu.VMEM)
    blocks = pl.pallas_call(
        split_columns,
        out_shape=b16((parts, rows_here, width)),
        in_specs=[pl.BlockSpec(memory_space=pl.ANY)],
        out_specs=pl.BlockSpec(memory_space=pl.ANY),
        scratch_shapes=[pltpu.SemaphoreType.DMA((parts,))],
    )(products)
    panel = lax.all_to_all(blocks, "blk", split_axis=0, concat_axis=0, tiled=True).reshape(rows, width)
    factor, high, low = pl.pallas_call(
        functools.partial(gram_factor, 64),
        out_shape=(f32((width, width)), b16((width, width)), b16((width, width))),
        in_specs=[in_smem, in_smem, in_vmem],
        out_specs=[in_vmem] * 3,
        scratch_shapes=[pltpu.VMEM((width, 2 * width), jnp.float32)],
        compiler_params=PARAMS,
    )(compat[0], sizes, panel)
    each = rows // groups
    whole = pl.BlockSpec((width, width), lambda k: (0, 0))
    ortho = pl.pallas_call(
        orthonormal_rows,
        grid=(groups,),
        out_shape=b16((1, rows, width)),
        in_specs=[in_smem, pl.BlockSpec((each, width), lambda k: (k, 0)), whole, whole],
        out_specs=pl.BlockSpec((1, each, width), lambda k: (0, k, 0)),
        compiler_params=PARAMS,
        cost_estimate=pl.CostEstimate(
            flops=4 * rows * width * width, bytes_accessed=4 * rows * width, transcendentals=0
        ),
    )(compat[0], panel, high, low)
    sites = lax.axis_size("seg")
    accumulated, by = factor, 1
    while by < sites:
        incoming = lax.ppermute(accumulated, "seg", [(i, i + by) for i in range(sites - by)])
        accumulated = pl.pallas_call(
            functools.partial(chained, by),
            out_shape=f32((width, width)),
            in_specs=[in_vmem] * 2,
            out_specs=in_vmem,
            compiler_params=PARAMS,
        )(accumulated, incoming)
        by *= 2
    return (ortho, accumulated[None, None])


def solution(mesh):
    in_specs = (P("seg", "blk", None), P("seg", "blk", None), P("seg", "blk"))
    out_specs = (P("seg", None, "blk"), P("seg", "blk", None, None))
    return jax.shard_map(local, mesh=mesh, in_specs=in_specs, out_specs=out_specs, check_vma=False)
```

```python
import functools
import math

import jax
import jax.numpy as jnp
from jax import lax
from jax.experimental import pallas as pl
from jax.experimental.pallas import tpu as pltpu
from jax.sharding import PartitionSpec as P

SHIFT = 0.05
HIGHEST = lax.Precision.HIGHEST
PARAMS = pltpu.CompilerParams(vmem_limit_bytes=48 << 20)
LANES = 128
SUB = 8


def wide(x, lanes):
    return jnp.concatenate([x] * (lanes // LANES), axis=1)


def split_columns(src, out):
    count, _, width = out.shape
    for k in range(count):
        out[k] = src[0, :, k * width : (k + 1) * width]


def factor_in_place(w, n, nb):
    row_at = lax.broadcasted_iota(jnp.int32, (SUB, LANES), 0)
    subs = nb // SUB
    for r0 in range(0, n, nb):
        p = [w[r0 + SUB * i : r0 + SUB * (i + 1), :] for i in range(subs)]
        for s in range(subs):
            cols = {}
            for i in range(s, subs):
                for c in range(SUB):
                    at = r0 + SUB * s + c
                    cols[i, c] = jnp.broadcast_to(p[i][:, at : at + 1], (SUB, LANES))
            pivots = jnp.ones((SUB, LANES), jnp.float32)
            for c in range(SUB):
                pivot = jnp.broadcast_to(cols[s, c][c : c + 1, :], (SUB, LANES))
                pivot = jnp.maximum(pivot, SHIFT * SHIFT)
                inverse = 1.0 / pivot
                pivots = jnp.where(row_at == c, pivot, pivots)
                row = jnp.broadcast_to(p[s][c : c + 1, :], p[s].shape)
                ahead = {
                    d: jnp.broadcast_to(cols[s, d][c : c + 1, :], (SUB, LANES)) for d in range(c + 1, SUB)
                }
                for i in range(s, subs):
                    times = cols[i, c] * inverse
                    if i == s:
                        if c == SUB - 1:
                            continue
                        times = jnp.where(row_at > c, times, 0.0)
                    p[i] = p[i] - wide(times, 2 * n) * row
                    for d in range(c + 1, SUB):
                        cols[i, d] = cols[i, d] - times * ahead[d]
            p[s] = p[s] * wide(lax.rsqrt(pivots), 2 * n)
        u = jnp.concatenate(p, axis=0)
        w[r0 : r0 + nb, :] = u
        end = r0 + nb
        if end < n:
            first = end // LANES * LANES
            last = n + -(-end // LANES) * LANES
            t = lax.dot_general(
                u[:, first:n],
                u[:, first:last],
                (((0,), (0,)), ((), ())),
                precision=HIGHEST,
                preferred_element_type=jnp.float32,
            )
            w[end:n, first:last] = w[end:n, first:last] - t[end - first :, :]


def gram_factor(nb, compat, size, panel, r_out, high_out, low_out, w):
    rows, n = panel.shape
    groups = compat.shape[1]
    each = rows // groups
    g = jnp.zeros((n, n), jnp.float32)
    for k in range(groups):
        block = panel[k * each : (k + 1) * each, :]
        part = lax.dot_general(block, block, (((0,), (0,)), ((), ())), preferred_element_type=jnp.float32)
        g = g + part * compat[0, k].astype(jnp.float32)
    i = lax.broadcasted_iota(jnp.int32, (n, n), 0)
    j = lax.broadcasted_iota(jnp.int32, (n, n), 1)
    live = jnp.logical_and(i < size[0, 0], j < size[0, 0])
    eye = (i == j).astype(jnp.float32)
    w[:, :n] = jnp.where(live, (1.0 + SHIFT) * g, 0.0) + (SHIFT * SHIFT) * eye
    w[:, n:] = eye
    factor_in_place(w, n, nb)
    r_out[...] = jnp.where(i <= j, w[:, :n], 0.0)
    inverse = jnp.where(jnp.logical_and(i >= j, live), w[:, n:], 0.0)
    high = inverse.astype(jnp.bfloat16)
    high_out[...] = high
    low_out[...] = (inverse - high.astype(jnp.float32)).astype(jnp.bfloat16)


def orthonormal_rows(compat, panel, high, low, out):
    dims = (((1,), (1,)), ((), ()))
    steps, groups = pl.num_programs(0), compat.shape[1]
    at = pl.program_id(0) * (groups // steps)
    each = panel.shape[0] * steps // groups
    for k in range(groups // steps):
        block = panel[k * each : (k + 1) * each, :]
        q = lax.dot_general(block, high[...], dims, preferred_element_type=jnp.float32)
        q = q + lax.dot_general(block, low[...], dims, preferred_element_type=jnp.float32)
        out[0, k * each : (k + 1) * each, :] = (q * compat[0, at + k].astype(jnp.float32)).astype(jnp.bfloat16)


def chained(by, own, incoming, out):
    later = lax.axis_index("seg") >= by

    @pl.when(later)
    def _():
        out[...] = jnp.dot(own[...], incoming[...], precision=HIGHEST, preferred_element_type=jnp.float32)

    @pl.when(jnp.logical_not(later))
    def _():
        out[...] = own[...]


def local(products, compat, sizes):
    parts = lax.axis_size("blk")
    rows_here, width = products.shape[1], products.shape[2] // parts
    rows = rows_here * parts
    groups = compat.shape[2]
    f32 = functools.partial(jax.ShapeDtypeStruct, dtype=jnp.float32)
    b16 = functools.partial(jax.ShapeDtypeStruct, dtype=jnp.bfloat16)
    in_smem = pl.BlockSpec(memory_space=pltpu.SMEM)
    in_vmem = pl.BlockSpec(memory_space=pltpu.VMEM)
    blocks = pl.pallas_call(
        split_columns,
        grid=(2,),
        out_shape=b16((parts, rows_here, width)),
        in_specs=[pl.BlockSpec((1, rows_here // 2, parts * width), lambda k: (0, k, 0))],
        out_specs=pl.BlockSpec((parts, rows_here // 2, width), lambda k: (0, k, 0)),
        compiler_params=PARAMS,
    )(products)
    panel = lax.all_to_all(blocks, "blk", split_axis=0, concat_axis=0, tiled=True).reshape(rows, width)
    factor, high, low = pl.pallas_call(
        functools.partial(gram_factor, 64),
        out_shape=(f32((width, width)), b16((width, width)), b16((width, width))),
        in_specs=[in_smem, in_smem, in_vmem],
        out_specs=[in_vmem] * 3,
        scratch_shapes=[pltpu.VMEM((width, 2 * width), jnp.float32)],
        compiler_params=PARAMS,
    )(compat[0], sizes, panel)
    steps = math.gcd(groups, 4)
    whole = pl.BlockSpec((width, width), lambda k: (0, 0))
    ortho = pl.pallas_call(
        orthonormal_rows,
        grid=(steps,),
        out_shape=b16((1, rows, width)),
        in_specs=[in_smem, pl.BlockSpec((rows // steps, width), lambda k: (k, 0)), whole, whole],
        out_specs=pl.BlockSpec((1, rows // steps, width), lambda k: (0, k, 0)),
        compiler_params=PARAMS,
        cost_estimate=pl.CostEstimate(
            flops=4 * rows * width * width, bytes_accessed=4 * rows * width, transcendentals=0
        ),
    )(compat[0], panel, high, low)
    sites = lax.axis_size("seg")
    accumulated, by = factor, 1
    while by < sites:
        incoming = lax.ppermute(accumulated, "seg", [(i, i + by) for i in range(sites - by)])
        accumulated = pl.pallas_call(
            functools.partial(chained, by),
            out_shape=f32((width, width)),
            in_specs=[in_vmem] * 2,
            out_specs=in_vmem,
            compiler_params=PARAMS,
        )(accumulated, incoming)
        by *= 2
    return (ortho, accumulated[None, None])


def solution(mesh):
    in_specs = (P("seg", "blk", None), P("seg", "blk", None), P("seg", "blk"))
    out_specs = (P("seg", None, "blk"), P("seg", "blk", None, None))
    return jax.shard_map(local, mesh=mesh, in_specs=in_specs, out_specs=out_specs, check_vma=False)
```

```python
import functools
import math

import jax
import jax.numpy as jnp
from jax import lax
from jax.experimental import pallas as pl
from jax.experimental.pallas import tpu as pltpu
from jax.sharding import PartitionSpec as P

SHIFT = 0.05
HIGHEST = lax.Precision.HIGHEST
PARAMS = pltpu.CompilerParams(vmem_limit_bytes=48 << 20)
LANES = 128
SUB = 8


def down(x, c):
    return jnp.broadcast_to(x[c : c + 1, :], (SUB, LANES))


def across(x, c):
    return jnp.broadcast_to(x[:, c : c + 1], (SUB, LANES))


def split_columns(src, out):
    count, _, width = out.shape
    for k in range(count):
        out[k] = src[0, :, k * width : (k + 1) * width]


def outer(u, first, last):
    high = u.astype(jnp.bfloat16)
    rest = u - high.astype(jnp.float32)
    mid = rest.astype(jnp.bfloat16)
    low = (rest - mid.astype(jnp.float32)).astype(jnp.bfloat16)
    left = jnp.concatenate([x[:, first:last] for x in (high, high, mid, high, mid, low)], axis=0)
    right = jnp.concatenate([high, mid, high, low, mid, high], axis=0)
    return lax.dot_general(left, right, (((0,), (0,)), ((), ())), preferred_element_type=jnp.float32)


def factor_in_place(w, n, step=16):
    row_at = lax.broadcasted_iota(jnp.int32, (SUB, LANES), 0)
    lanes = 2 * n // LANES
    p = {}
    for r0 in range(0, n, step):
        half, base = r0 // LANES, r0 % LANES
        end = r0 + step
        act = range(half, min(lanes, half + n // LANES + 1))
        held = range(r0, min(end + step, n), SUB)
        for r in held:
            for t in act:
                if (r, t) not in p:
                    p[r, t] = w[r : r + SUB, t * LANES : (t + 1) * LANES]
        cols = {}
        for r in held:
            for c in range(min(step, r - r0 + SUB)):
                cols[r, c] = across(p[r, half], base + c)
        pivots = {r: jnp.ones((SUB, LANES), jnp.float32) for r in range(r0, end, SUB)}
        for c in range(step):
            own, at = r0 + c // SUB * SUB, c % SUB
            pivot = jnp.maximum(down(cols[own, c], at), SHIFT * SHIFT)
            inverse = 1.0 / pivot
            pivots[own] = jnp.where(row_at == at, pivot, pivots[own])
            row = {t: down(p[own, t], at) for t in act}
            ahead = {d: down(cols[r0 + d // SUB * SUB, c], d % SUB) for d in range(c + 1, step)}
            for r in held:
                if r < own or (r == own and at == SUB - 1):
                    continue
                x = cols[r, c]
                if r == own:
                    x = jnp.where(row_at > at, x, 0.0)
                times = x * inverse
                for d in range(c + 1, step):
                    if (r, d) not in cols:
                        continue
                    if d == c + 1 and r == r0 + d // SUB * SUB:
                        cols[r, d] = cols[r, d] - (x * ahead[d]) * inverse
                    else:
                        cols[r, d] = cols[r, d] - times * ahead[d]
                for t in act:
                    p[r, t] = p[r, t] - times * row[t]
        for r in range(r0, end, SUB):
            scale = lax.rsqrt(pivots[r])
            for t in act:
                p[r, t] = p[r, t] * scale
                w[r : r + SUB, t * LANES : (t + 1) * LANES] = p[r, t]
        below = end + step
        if below < n:
            first, last = end // LANES, act[-1] + 1
            u = jnp.concatenate(
                [
                    jnp.concatenate([p[r, t] for t in range(first, last)], axis=1)
                    for r in range(r0, end, SUB)
                ],
                axis=0,
            )
            skip = below // LANES
            update = outer(u, (skip - first) * LANES, n - first * LANES)
            cut = slice(first * LANES, last * LANES)
            w[below:n, cut] = w[below:n, cut] - update[below - skip * LANES :, :]
        p = {at: value for at, value in p.items() if at[0] >= end}


def gram_factor(compat, size, panel, r_out, high_out, low_out, w):
    rows, n = panel.shape
    groups = compat.shape[1]
    each = rows // groups
    g = jnp.zeros((n, n), jnp.float32)
    for k in range(groups):
        block = panel[k * each : (k + 1) * each, :]
        part = lax.dot_general(block, block, (((0,), (0,)), ((), ())), preferred_element_type=jnp.float32)
        g = g + part * compat[0, k].astype(jnp.float32)
    i = lax.broadcasted_iota(jnp.int32, (n, n), 0)
    j = lax.broadcasted_iota(jnp.int32, (n, n), 1)
    live = jnp.logical_and(i < size[0, 0], j < size[0, 0])
    eye = (i == j).astype(jnp.float32)
    w[:, :n] = jnp.where(live, (1.0 + SHIFT) * g, 0.0) + (SHIFT * SHIFT) * eye
    w[:, n:] = eye
    factor_in_place(w, n)
    r_out[...] = jnp.where(i <= j, w[:, :n], 0.0)
    inverse = jnp.where(jnp.logical_and(i >= j, live), w[:, n:], 0.0)
    high = inverse.astype(jnp.bfloat16)
    high_out[...] = high
    low_out[...] = (inverse - high.astype(jnp.float32)).astype(jnp.bfloat16)


def orthonormal_rows(compat, panel, high, low, out):
    dims = (((1,), (1,)), ((), ()))
    steps, groups = pl.num_programs(0), compat.shape[1]
    at = pl.program_id(0) * (groups // steps)
    each = panel.shape[0] * steps // groups
    for k in range(groups // steps):
        block = panel[k * each : (k + 1) * each, :]
        q = lax.dot_general(block, high[...], dims, preferred_element_type=jnp.float32)
        q = q + lax.dot_general(block, low[...], dims, preferred_element_type=jnp.float32)
        out[0, k * each : (k + 1) * each, :] = (q * compat[0, at + k].astype(jnp.float32)).astype(jnp.bfloat16)


def chained(by, own, incoming, out):
    later = lax.axis_index("seg") >= by

    @pl.when(later)
    def _():
        out[...] = jnp.dot(own[...], incoming[...], precision=HIGHEST, preferred_element_type=jnp.float32)

    @pl.when(jnp.logical_not(later))
    def _():
        out[...] = own[...]


def local(products, compat, sizes):
    parts = lax.axis_size("blk")
    rows_here, width = products.shape[1], products.shape[2] // parts
    rows = rows_here * parts
    groups = compat.shape[2]
    f32 = functools.partial(jax.ShapeDtypeStruct, dtype=jnp.float32)
    b16 = functools.partial(jax.ShapeDtypeStruct, dtype=jnp.bfloat16)
    in_smem = pl.BlockSpec(memory_space=pltpu.SMEM)
    in_vmem = pl.BlockSpec(memory_space=pltpu.VMEM)
    blocks = pl.pallas_call(
        split_columns,
        grid=(2,),
        out_shape=b16((parts, rows_here, width)),
        in_specs=[pl.BlockSpec((1, rows_here // 2, parts * width), lambda k: (0, k, 0))],
        out_specs=pl.BlockSpec((parts, rows_here // 2, width), lambda k: (0, k, 0)),
        compiler_params=PARAMS,
    )(products)
    panel = lax.all_to_all(blocks, "blk", split_axis=0, concat_axis=0, tiled=True).reshape(rows, width)
    factor, high, low = pl.pallas_call(
        gram_factor,
        out_shape=(f32((width, width)), b16((width, width)), b16((width, width))),
        in_specs=[in_smem, in_smem, in_vmem],
        out_specs=[in_vmem] * 3,
        scratch_shapes=[pltpu.VMEM((width, 2 * width), jnp.float32)],
        compiler_params=PARAMS,
    )(compat[0], sizes, panel)
    steps = math.gcd(groups, 4)
    whole = pl.BlockSpec((width, width), lambda k: (0, 0))
    ortho = pl.pallas_call(
        orthonormal_rows,
        grid=(steps,),
        out_shape=b16((1, rows, width)),
        in_specs=[in_smem, pl.BlockSpec((rows // steps, width), lambda k: (k, 0)), whole, whole],
        out_specs=pl.BlockSpec((1, rows // steps, width), lambda k: (0, k, 0)),
        compiler_params=PARAMS,
        cost_estimate=pl.CostEstimate(
            flops=4 * rows * width * width, bytes_accessed=4 * rows * width, transcendentals=0
        ),
    )(compat[0], panel, high, low)
    sites = lax.axis_size("seg")
    accumulated, by = factor, 1
    while by < sites:
        incoming = lax.ppermute(accumulated, "seg", [(i, i + by) for i in range(sites - by)])
        accumulated = pl.pallas_call(
            functools.partial(chained, by),
            out_shape=f32((width, width)),
            in_specs=[in_vmem] * 2,
            out_specs=in_vmem,
            compiler_params=PARAMS,
        )(accumulated, incoming)
        by *= 2
    return (ortho, accumulated[None, None])


def solution(mesh):
    in_specs = (P("seg", "blk", None), P("seg", "blk", None), P("seg", "blk"))
    out_specs = (P("seg", None, "blk"), P("seg", "blk", None, None))
    return jax.shard_map(local, mesh=mesh, in_specs=in_specs, out_specs=out_specs, check_vma=False)
```

```python
import functools
import math

import jax
import jax.numpy as jnp
from jax import lax
from jax.experimental import pallas as pl
from jax.experimental.pallas import tpu as pltpu
from jax.sharding import PartitionSpec as P

SHIFT = 0.05
HIGHEST = lax.Precision.HIGHEST
PARAMS = pltpu.CompilerParams(vmem_limit_bytes=48 << 20)
LANES = 128
SUB = 8


def down(x, c):
    return jnp.broadcast_to(x[c : c + 1, :], (SUB, LANES))


def across(x, c):
    return jnp.broadcast_to(x[:, c : c + 1], (SUB, LANES))


def split_columns(src, out, rows, blocks, arrived, sent):
    count, total, width = out.shape
    parts = arrived.shape[0]
    each = total // parts
    cuts = [pl.ds(i * each, each) for i in range(parts)]
    reads = [pltpu.make_async_copy(src.at[0, cut], rows.at[cut], arrived.at[i]) for i, cut in enumerate(cuts)]
    writes = [pltpu.make_async_copy(blocks.at[:, cut], out.at[:, cut], sent.at[i]) for i, cut in enumerate(cuts)]
    for read in reads:
        read.start()
    for cut, read, write in zip(cuts, reads, writes):
        read.wait()
        for k in range(count):
            blocks[k, cut, :] = rows[cut, k * width : (k + 1) * width]
        write.start()
    for write in writes:
        write.wait()


def outer(u, first, last):
    high = u.astype(jnp.bfloat16)
    rest = u - high.astype(jnp.float32)
    mid = rest.astype(jnp.bfloat16)
    low = (rest - mid.astype(jnp.float32)).astype(jnp.bfloat16)
    left = jnp.concatenate([x[:, first:last] for x in (high, high, mid, high, mid, low)], axis=0)
    right = jnp.concatenate([high, mid, high, low, mid, high], axis=0)
    return lax.dot_general(left, right, (((0,), (0,)), ((), ())), preferred_element_type=jnp.float32)


def factor_in_place(w, n, step=16):
    row_at = lax.broadcasted_iota(jnp.int32, (SUB, LANES), 0)
    lanes = 2 * n // LANES
    p = {}
    for r0 in range(0, n, step):
        half, base = r0 // LANES, r0 % LANES
        end = r0 + step
        act = range(half, min(lanes, half + n // LANES + 1))
        held = range(r0, min(end + step, n), SUB)
        for r in held:
            for t in act:
                if (r, t) not in p:
                    p[r, t] = w[r : r + SUB, t * LANES : (t + 1) * LANES]
        cols = {}
        for r in held:
            for c in range(min(step, r - r0 + SUB)):
                cols[r, c] = across(p[r, half], base + c)
        pivots = {r: jnp.ones((SUB, LANES), jnp.float32) for r in range(r0, end, SUB)}
        for c in range(step):
            own, at = r0 + c // SUB * SUB, c % SUB
            pivot = jnp.maximum(down(cols[own, c], at), SHIFT * SHIFT)
            inverse = 1.0 / pivot
            pivots[own] = jnp.where(row_at == at, pivot, pivots[own])
            row = {t: down(p[own, t], at) for t in act}
            ahead = {d: down(cols[r0 + d // SUB * SUB, c], d % SUB) for d in range(c + 1, step)}
            for r in held:
                if r < own or (r == own and at == SUB - 1):
                    continue
                x = cols[r, c]
                if r == own:
                    x = jnp.where(row_at > at, x, 0.0)
                times = x * inverse
                for d in range(c + 1, step):
                    if (r, d) not in cols:
                        continue
                    if d == c + 1 and r == r0 + d // SUB * SUB:
                        cols[r, d] = cols[r, d] - (x * ahead[d]) * inverse
                    else:
                        cols[r, d] = cols[r, d] - times * ahead[d]
                for t in act:
                    p[r, t] = p[r, t] - times * row[t]
        for r in range(r0, end, SUB):
            scale = lax.rsqrt(pivots[r])
            for t in act:
                p[r, t] = p[r, t] * scale
                w[r : r + SUB, t * LANES : (t + 1) * LANES] = p[r, t]
        below = end + step
        if below < n:
            first, last = end // LANES, act[-1] + 1
            u = jnp.concatenate(
                [
                    jnp.concatenate([p[r, t] for t in range(first, last)], axis=1)
                    for r in range(r0, end, SUB)
                ],
                axis=0,
            )
            skip = below // LANES
            update = outer(u, (skip - first) * LANES, n - first * LANES)
            cut = slice(first * LANES, last * LANES)
            w[below:n, cut] = w[below:n, cut] - update[below - skip * LANES :, :]
        p = {at: value for at, value in p.items() if at[0] >= end}


def pack(r, out):
    n = r.shape[0]
    q = n // 4
    out[:q, :] = r[:q, :]
    out[q : 2 * q, :] = r[q : 2 * q, :]
    out[q : 2 * q, :q] = r[3 * q :, 3 * q :]
    out[2 * q :, : 2 * q] = r[2 * q : 2 * q + q // 2, 2 * q :]
    out[2 * q :, 2 * q :] = r[2 * q + q // 2 : 3 * q, 2 * q :]


def unpack(packed, r):
    n = r.shape[0]
    q = n // 4
    r[:q, :] = packed[:q, :]
    r[q : 2 * q, :] = packed[q : 2 * q, :]
    r[q : 2 * q, :q] = jnp.zeros((q, q), r.dtype)
    r[2 * q :, : 2 * q] = jnp.zeros((2 * q, 2 * q), r.dtype)
    r[2 * q : 2 * q + q // 2, 2 * q :] = packed[2 * q :, : 2 * q]
    r[2 * q + q // 2 : 3 * q, 2 * q :] = packed[2 * q :, 2 * q :]
    r[3 * q :, 2 * q : 3 * q] = jnp.zeros((q, q), r.dtype)
    r[3 * q :, 3 * q :] = packed[q : 2 * q, :q]


def gram_factor(compat, size, panel, r_out, packed_out, high_out, low_out, w):
    rows, n = panel.shape
    groups = compat.shape[1]
    each = rows // groups
    g = jnp.zeros((n, n), jnp.float32)
    for k in range(groups):
        block = panel[k * each : (k + 1) * each, :]
        part = lax.dot_general(block, block, (((0,), (0,)), ((), ())), preferred_element_type=jnp.float32)
        g = g + part * compat[0, k].astype(jnp.float32)
    i = lax.broadcasted_iota(jnp.int32, (n, n), 0)
    j = lax.broadcasted_iota(jnp.int32, (n, n), 1)
    live = jnp.logical_and(i < size[0, 0], j < size[0, 0])
    eye = (i == j).astype(jnp.float32)
    w[:, :n] = jnp.where(live, (1.0 + SHIFT) * g, 0.0) + (SHIFT * SHIFT) * eye
    w[:, n:] = eye
    factor_in_place(w, n)
    r_out[...] = jnp.where(i <= j, w[:, :n], 0.0)
    pack(r_out, packed_out)
    inverse = jnp.where(jnp.logical_and(i >= j, live), w[:, n:], 0.0)
    high = inverse.astype(jnp.bfloat16)
    high_out[...] = high
    low_out[...] = (inverse - high.astype(jnp.float32)).astype(jnp.bfloat16)


def orthonormal_rows(compat, panel, high, low, out):
    dims = (((1,), (1,)), ((), ()))
    steps, groups = pl.num_programs(0), compat.shape[1]
    at = pl.program_id(0) * (groups // steps)
    each = panel.shape[0] * steps // groups
    for k in range(groups // steps):
        block = panel[k * each : (k + 1) * each, :]
        q = lax.dot_general(block, high[...], dims, preferred_element_type=jnp.float32)
        q = q + lax.dot_general(block, low[...], dims, preferred_element_type=jnp.float32)
        out[0, k * each : (k + 1) * each, :] = (q * compat[0, at + k].astype(jnp.float32)).astype(jnp.bfloat16)


def chained(by, own, incoming, out, packed_out, before):
    later = lax.axis_index("seg") >= by

    @pl.when(later)
    def _():
        unpack(incoming, before)
        h = own.shape[0] // 2
        dot = functools.partial(jnp.dot, precision=HIGHEST, preferred_element_type=jnp.float32)
        out[:h, :] = dot(own[:h, :], before[...])
        out[h:, :h] = jnp.zeros((h, h), jnp.float32)
        out[h:, h:] = dot(own[h:, h:], before[h:, h:])

    @pl.when(jnp.logical_not(later))
    def _():
        out[...] = own[...]

    pack(out, packed_out)


def local(products, compat, sizes):
    parts = lax.axis_size("blk")
    rows_here, width = products.shape[1], products.shape[2] // parts
    rows = rows_here * parts
    groups = compat.shape[2]
    f32 = functools.partial(jax.ShapeDtypeStruct, dtype=jnp.float32)
    b16 = functools.partial(jax.ShapeDtypeStruct, dtype=jnp.bfloat16)
    in_smem = pl.BlockSpec(memory_space=pltpu.SMEM)
    in_vmem = pl.BlockSpec(memory_space=pltpu.VMEM)
    in_hbm = pl.BlockSpec(memory_space=pltpu.MemorySpace.HBM)
    pieces = 4
    blocks = pl.pallas_call(
        split_columns,
        out_shape=b16((parts, rows_here, width)),
        in_specs=[in_hbm],
        out_specs=in_hbm,
        scratch_shapes=[
            pltpu.VMEM((rows_here, parts * width), jnp.bfloat16),
            pltpu.VMEM((parts, rows_here, width), jnp.bfloat16),
            pltpu.SemaphoreType.DMA((pieces,)),
            pltpu.SemaphoreType.DMA((pieces,)),
        ],
        compiler_params=pltpu.CompilerParams(vmem_limit_bytes=62 << 20),
    )(products)
    panel = lax.all_to_all(blocks, "blk", split_axis=0, concat_axis=0, tiled=True).reshape(rows, width)
    packed_rows = 5 * width // 8
    factor, packed, high, low = pl.pallas_call(
        gram_factor,
        out_shape=(f32((width, width)), f32((packed_rows, width)), b16((width, width)), b16((width, width))),
        in_specs=[in_smem, in_smem, in_vmem],
        out_specs=[in_vmem] * 4,
        scratch_shapes=[pltpu.VMEM((width, 2 * width), jnp.float32)],
        compiler_params=PARAMS,
    )(compat[0], sizes, panel)
    steps = math.gcd(groups, 4)
    whole = pl.BlockSpec((width, width), lambda k: (0, 0))
    ortho = pl.pallas_call(
        orthonormal_rows,
        grid=(steps,),
        out_shape=b16((1, rows, width)),
        in_specs=[in_smem, pl.BlockSpec((rows // steps, width), lambda k: (k, 0)), whole, whole],
        out_specs=pl.BlockSpec((1, rows // steps, width), lambda k: (0, k, 0)),
        compiler_params=PARAMS,
        cost_estimate=pl.CostEstimate(
            flops=4 * rows * width * width, bytes_accessed=4 * rows * width, transcendentals=0
        ),
    )(compat[0], panel, high, low)
    sites = lax.axis_size("seg")
    accumulated, by = factor, 1
    while by < sites:
        incoming = lax.ppermute(packed, "seg", [(i, (i + by) % sites) for i in range(sites)])
        accumulated, packed = pl.pallas_call(
            functools.partial(chained, by),
            out_shape=(f32((width, width)), f32((packed_rows, width))),
            in_specs=[in_vmem] * 2,
            out_specs=[in_vmem] * 2,
            scratch_shapes=[pltpu.VMEM((width, width), jnp.float32)],
            compiler_params=PARAMS,
        )(accumulated, incoming)
        by *= 2
    return (ortho, accumulated[None, None])


def solution(mesh):
    in_specs = (P("seg", "blk", None), P("seg", "blk", None), P("seg", "blk"))
    out_specs = (P("seg", None, "blk"), P("seg", "blk", None, None))
    return jax.shard_map(local, mesh=mesh, in_specs=in_specs, out_specs=out_specs, check_vma=False)
```

```python
import functools

import jax
import jax.numpy as jnp
from jax import lax
from jax.experimental import pallas as pl
from jax.experimental.pallas import tpu as pltpu
from jax.sharding import PartitionSpec as P

SHIFT = 0.05
HIGHEST = lax.Precision.HIGHEST
PARAMS = pltpu.CompilerParams(vmem_limit_bytes=48 << 20)
LANES = 128
SUB = 8
FAR, NEAR, LATE = 4, 3, 3


def down(x, c):
    return jnp.broadcast_to(x[c : c + 1, :], (SUB, LANES))


def across(x, c):
    return jnp.broadcast_to(x[:, c : c + 1], (SUB, LANES))


def split_columns(src, *refs):
    *outs, rows, arrived = refs
    total, width = outs[0].shape
    parts = arrived.shape[0]
    each = total // parts
    me = lax.axis_index("blk")
    cuts = [pl.ds(i * each, each) for i in range(parts)]
    reads = [pltpu.make_async_copy(src.at[0, cut], rows.at[cut], arrived.at[i]) for i, cut in enumerate(cuts)]
    for read in reads:
        read.start()
    for cut, read in zip(cuts, reads):
        read.wait()
        for r, out in enumerate(outs):
            out[cut, :] = rows[cut, pl.ds(pl.multiple_of((me ^ r) * width, width), width)]


def outer(u, first, last):
    high = u.astype(jnp.bfloat16)
    rest = u - high.astype(jnp.float32)
    mid = rest.astype(jnp.bfloat16)
    low = (rest - mid.astype(jnp.float32)).astype(jnp.bfloat16)
    left = jnp.concatenate([x[:, first:last] for x in (high, high, mid, high, mid, low)], axis=0)
    right = jnp.concatenate([high, mid, high, low, mid, high], axis=0)
    return lax.dot_general(left, right, (((0,), (0,)), ((), ())), preferred_element_type=jnp.float32)


def factor_in_place(w, n, step=16):
    row_at = lax.broadcasted_iota(jnp.int32, (SUB, LANES), 0)
    lanes = 2 * n // LANES
    p = {}
    for r0 in range(0, n, step):
        half, base = r0 // LANES, r0 % LANES
        end = r0 + step
        act = range(half, min(lanes, half + n // LANES + 1))
        held = range(r0, min(end + step, n), SUB)
        for r in held:
            for t in act:
                if (r, t) not in p:
                    p[r, t] = w[r : r + SUB, t * LANES : (t + 1) * LANES]
        cols = {}
        for r in held:
            for c in range(min(step, r - r0 + SUB)):
                cols[r, c] = across(p[r, half], base + c)
        pivots = {r: jnp.ones((SUB, LANES), jnp.float32) for r in range(r0, end, SUB)}
        for c in range(step):
            own, at = r0 + c // SUB * SUB, c % SUB
            pivot = jnp.maximum(down(cols[own, c], at), SHIFT * SHIFT)
            inverse = 1.0 / pivot
            pivots[own] = jnp.where(row_at == at, pivot, pivots[own])
            row = {t: down(p[own, t], at) for t in act}
            ahead = {d: down(cols[r0 + d // SUB * SUB, c], d % SUB) for d in range(c + 1, step)}
            for r in held:
                if r < own or (r == own and at == SUB - 1):
                    continue
                x = cols[r, c]
                if r == own:
                    x = jnp.where(row_at > at, x, 0.0)
                times = x * inverse
                for d in range(c + 1, step):
                    if (r, d) not in cols:
                        continue
                    if d == c + 1 and r == r0 + d // SUB * SUB:
                        cols[r, d] = cols[r, d] - (x * ahead[d]) * inverse
                    else:
                        cols[r, d] = cols[r, d] - times * ahead[d]
                for t in act:
                    p[r, t] = p[r, t] - times * row[t]
        for r in range(r0, end, SUB):
            scale = lax.rsqrt(pivots[r])
            for t in act:
                p[r, t] = p[r, t] * scale
                w[r : r + SUB, t * LANES : (t + 1) * LANES] = p[r, t]
        below = end + step
        if below < n:
            first, last = end // LANES, act[-1] + 1
            u = jnp.concatenate(
                [
                    jnp.concatenate([p[r, t] for t in range(first, last)], axis=1)
                    for r in range(r0, end, SUB)
                ],
                axis=0,
            )
            skip = below // LANES
            update = outer(u, (skip - first) * LANES, n - first * LANES)
            cut = slice(first * LANES, last * LANES)
            w[below:n, cut] = w[below:n, cut] - update[below - skip * LANES :, :]
        p = {at: value for at, value in p.items() if at[0] >= end}


def pack(r, out):
    n = r.shape[0]
    q = n // 4
    out[:q, :] = r[:q, :]
    out[q : 2 * q, :] = r[q : 2 * q, :]
    out[q : 2 * q, :q] = r[3 * q :, 3 * q :]
    out[2 * q :, : 2 * q] = r[2 * q : 2 * q + q // 2, 2 * q :]
    out[2 * q :, 2 * q :] = r[2 * q + q // 2 : 3 * q, 2 * q :]


def unpack(packed, r):
    n = r.shape[0]
    q = n // 4
    r[:q, :] = packed[:q, :]
    r[q : 2 * q, :] = packed[q : 2 * q, :]
    r[q : 2 * q, :q] = jnp.zeros((q, q), r.dtype)
    r[2 * q :, : 2 * q] = jnp.zeros((2 * q, 2 * q), r.dtype)
    r[2 * q : 2 * q + q // 2, 2 * q :] = packed[2 * q :, : 2 * q]
    r[2 * q + q // 2 : 3 * q, 2 * q :] = packed[2 * q :, 2 * q :]
    r[3 * q :, 2 * q : 3 * q] = jnp.zeros((q, q), r.dtype)
    r[3 * q :, 3 * q :] = packed[q : 2 * q, :q]


def sender_allows(compat, r, each, rows):
    sender = lax.axis_index("blk") ^ r
    return compat[0, sender * each // (rows // compat.shape[1])].astype(jnp.float32)


def gram_of(rounds, rows, compat, blocks):
    total = None
    for r, block in zip(rounds, blocks):
        x = block[...]
        part = lax.dot_general(x, x, (((0,), (0,)), ((), ())), preferred_element_type=jnp.float32)
        part = part * sender_allows(compat, r, x.shape[0], rows)
        total = part if total is None else total + part
    return total


def gram_part(rounds, rows, compat, *refs):
    refs[-1][...] = gram_of(rounds, rows, compat, refs[:-1])


def gram_factor(rounds, rows, compat, size, before, *refs):
    *blocks, r_out, packed_out, high_out, low_out, w = refs
    n = before.shape[0]
    g = before[...] + gram_of(rounds, rows, compat, blocks)
    i = lax.broadcasted_iota(jnp.int32, (n, n), 0)
    j = lax.broadcasted_iota(jnp.int32, (n, n), 1)
    live = jnp.logical_and(i < size[0, 0], j < size[0, 0])
    eye = (i == j).astype(jnp.float32)
    w[:, :n] = jnp.where(live, (1.0 + SHIFT) * g, 0.0) + (SHIFT * SHIFT) * eye
    w[:, n:] = eye
    factor_in_place(w, n)
    r_out[...] = jnp.where(i <= j, w[:, :n], 0.0)
    pack(r_out, packed_out)
    inverse = jnp.where(jnp.logical_and(i >= j, live), w[:, n:], 0.0)
    high = inverse.astype(jnp.bfloat16)
    high_out[...] = high
    low_out[...] = (inverse - high.astype(jnp.float32)).astype(jnp.bfloat16)


def orthonormal_rows(rounds, rows, compat, high, low, *refs):
    *blocks, out, results, sent = refs
    dims = (((1,), (1,)), ((), ()))
    each = blocks[0].shape[0]
    me = lax.axis_index("blk")
    copies = []
    for i, (r, block) in enumerate(zip(rounds, blocks)):
        x = block[...]
        q = lax.dot_general(x, high[...], dims, preferred_element_type=jnp.float32)
        q = q + lax.dot_general(x, low[...], dims, preferred_element_type=jnp.float32)
        results[i] = (q * sender_allows(compat, r, each, rows)).astype(jnp.bfloat16)
        place = pl.ds(pl.multiple_of((me ^ r) * each, each), each)
        copies.append(pltpu.make_async_copy(results.at[i], out.at[0, place], sent.at[i]))
        copies[-1].start()
    for copy in copies:
        copy.wait()


def chained(by, own, incoming, out, packed_out, before):
    later = lax.axis_index("seg") >= by

    @pl.when(later)
    def _():
        unpack(incoming, before)
        h = own.shape[0] // 2
        dot = functools.partial(jnp.dot, precision=HIGHEST, preferred_element_type=jnp.float32)
        out[:h, :] = dot(own[:h, :], before[...])
        out[h:, :h] = jnp.zeros((h, h), jnp.float32)
        out[h:, h:] = dot(own[h:, h:], before[h:, h:])

    @pl.when(jnp.logical_not(later))
    def _():
        out[...] = own[...]

    pack(out, packed_out)


def local(products, compat, sizes):
    parts = lax.axis_size("blk")
    rows_here, width = products.shape[1], products.shape[2] // parts
    rows = rows_here * parts
    f32 = functools.partial(jax.ShapeDtypeStruct, dtype=jnp.float32)
    b16 = functools.partial(jax.ShapeDtypeStruct, dtype=jnp.bfloat16)
    in_smem = pl.BlockSpec(memory_space=pltpu.SMEM)
    in_vmem = pl.BlockSpec(memory_space=pltpu.VMEM)
    in_hbm = pl.BlockSpec(memory_space=pltpu.MemorySpace.HBM)
    pieces = 4
    blocks = pl.pallas_call(
        split_columns,
        out_shape=[b16((rows_here, width))] * parts,
        in_specs=[in_hbm],
        out_specs=[in_vmem] * parts,
        scratch_shapes=[
            pltpu.VMEM((rows_here, parts * width), jnp.bfloat16),
            pltpu.SemaphoreType.DMA((pieces,)),
        ],
        compiler_params=PARAMS,
    )(products)
    half, quarter = parts // 2, parts // 4
    far = [r for pair in zip(range(half, half + quarter), range(half + quarter, parts)) for r in pair]
    near = [*range(quarter, half), *range(1, quarter)]
    got = {0: blocks[0]}
    for order, window in ((far, FAR), (near, NEAR)):
        for i, r in enumerate(order):
            block = blocks[r]
            if i >= window:
                block, _ = lax.optimization_barrier((block, got[order[i - window]]))
            got[r] = lax.ppermute(block, "blk", [(k, k ^ r) for k in range(parts)])
    early, late = [0, *near, *far[: -LATE]], far[-LATE:]
    partial = pl.pallas_call(
        functools.partial(gram_part, early, rows),
        out_shape=f32((width, width)),
        in_specs=[in_smem] + [in_vmem] * len(early),
        out_specs=in_vmem,
        compiler_params=PARAMS,
    )(compat[0], *[got[r] for r in early])
    packed_rows = 5 * width // 8
    factor, packed, high, low = pl.pallas_call(
        functools.partial(gram_factor, late, rows),
        out_shape=(f32((width, width)), f32((packed_rows, width)), b16((width, width)), b16((width, width))),
        in_specs=[in_smem, in_smem] + [in_vmem] * (1 + len(late)),
        out_specs=[in_vmem] * 4,
        scratch_shapes=[pltpu.VMEM((width, 2 * width), jnp.float32)],
        compiler_params=PARAMS,
    )(compat[0], sizes, partial, *[got[r] for r in late])
    rounds = sorted(got)
    ortho = pl.pallas_call(
        functools.partial(orthonormal_rows, rounds, rows),
        out_shape=b16((1, rows, width)),
        in_specs=[in_smem] + [in_vmem] * (2 + parts),
        out_specs=in_hbm,
        scratch_shapes=[
            pltpu.VMEM((parts, rows_here, width), jnp.bfloat16),
            pltpu.SemaphoreType.DMA((parts,)),
        ],
        compiler_params=PARAMS,
        cost_estimate=pl.CostEstimate(
            flops=4 * rows * width * width, bytes_accessed=4 * rows * width, transcendentals=0
        ),
    )(compat[0], high, low, *[got[r] for r in rounds])
    sites = lax.axis_size("seg")
    accumulated, by = factor, 1
    while by < sites:
        incoming = lax.ppermute(packed, "seg", [(i, (i + by) % sites) for i in range(sites)])
        accumulated, packed = pl.pallas_call(
            functools.partial(chained, by),
            out_shape=(f32((width, width)), f32((packed_rows, width))),
            in_specs=[in_vmem] * 2,
            out_specs=[in_vmem] * 2,
            scratch_shapes=[pltpu.VMEM((width, width), jnp.float32)],
            compiler_params=PARAMS,
        )(accumulated, incoming)
        by *= 2
    return (ortho, accumulated[None, None])


def solution(mesh):
    in_specs = (P("seg", "blk", None), P("seg", "blk", None), P("seg", "blk"))
    out_specs = (P("seg", None, "blk"), P("seg", "blk", None, None))
    return jax.shard_map(local, mesh=mesh, in_specs=in_specs, out_specs=out_specs, check_vma=False)
```

```python
import functools

import jax
import jax.numpy as jnp
from jax import lax
from jax.experimental import pallas as pl
from jax.experimental.pallas import tpu as pltpu
from jax.sharding import PartitionSpec as P

SHIFT = 0.05
HIGHEST = lax.Precision.HIGHEST
PARAMS = pltpu.CompilerParams(vmem_limit_bytes=48 << 20)
LANES = 128
SUB = 8
FAR, NEAR, LATE, AHEAD = 5, 3, 3, 3


def down(x, c):
    return jnp.broadcast_to(x[c : c + 1, :], (SUB, LANES))


def across(x, c):
    return jnp.broadcast_to(x[:, c : c + 1], (SUB, LANES))


def split_columns(wanted, src, *refs):
    *outs, rows, arrived = refs
    total = rows.shape[0]
    parts = arrived.shape[0]
    each = total // parts
    width = rows.shape[1] // lax.axis_size("blk")
    me = lax.axis_index("blk")
    cuts = [pl.ds(i * each, each) for i in range(parts)]
    reads = [pltpu.make_async_copy(src.at[0, cut], rows.at[cut], arrived.at[i]) for i, cut in enumerate(cuts)]
    for read in reads:
        read.start()
    for cut, read in zip(cuts, reads):
        read.wait()
        for (r, first, count), out in zip(wanted, outs):
            at = pl.multiple_of((me ^ r) * width + first, LANES)
            out[cut, :] = rows[cut, pl.ds(at, count)]


def outer(u, first, last):
    high = u.astype(jnp.bfloat16)
    rest = u - high.astype(jnp.float32)
    mid = rest.astype(jnp.bfloat16)
    low = (rest - mid.astype(jnp.float32)).astype(jnp.bfloat16)
    left = jnp.concatenate([x[:, first:last] for x in (high, high, mid, high, mid, low)], axis=0)
    right = jnp.concatenate([high, mid, high, low, mid, high], axis=0)
    return lax.dot_general(left, right, (((0,), (0,)), ((), ())), preferred_element_type=jnp.float32)


def factor_in_place(w, n, step=16):
    row_at = lax.broadcasted_iota(jnp.int32, (SUB, LANES), 0)
    lanes = 2 * n // LANES
    p = {}
    for r0 in range(0, n, step):
        half, base = r0 // LANES, r0 % LANES
        end = r0 + step
        act = range(half, min(lanes, half + n // LANES + 1))
        held = range(r0, min(end + step, n), SUB)
        for r in held:
            for t in act:
                if (r, t) not in p:
                    p[r, t] = w[r : r + SUB, t * LANES : (t + 1) * LANES]
        cols = {}
        for r in held:
            for c in range(min(step, r - r0 + SUB)):
                cols[r, c] = across(p[r, half], base + c)
        pivots = {r: jnp.ones((SUB, LANES), jnp.float32) for r in range(r0, end, SUB)}
        for c in range(step):
            own, at = r0 + c // SUB * SUB, c % SUB
            pivot = jnp.maximum(down(cols[own, c], at), SHIFT * SHIFT)
            inverse = 1.0 / pivot
            pivots[own] = jnp.where(row_at == at, pivot, pivots[own])
            row = {t: down(p[own, t], at) for t in act}
            ahead = {d: down(cols[r0 + d // SUB * SUB, c], d % SUB) for d in range(c + 1, step)}
            for r in held:
                if r < own or (r == own and at == SUB - 1):
                    continue
                x = cols[r, c]
                if r == own:
                    x = jnp.where(row_at > at, x, 0.0)
                times = x * inverse
                for d in range(c + 1, step):
                    if (r, d) not in cols:
                        continue
                    if d == c + 1 and r == r0 + d // SUB * SUB:
                        cols[r, d] = cols[r, d] - (x * ahead[d]) * inverse
                    else:
                        cols[r, d] = cols[r, d] - times * ahead[d]
                for t in act:
                    p[r, t] = p[r, t] - times * row[t]
        for r in range(r0, end, SUB):
            scale = lax.rsqrt(pivots[r])
            for t in act:
                p[r, t] = p[r, t] * scale
                w[r : r + SUB, t * LANES : (t + 1) * LANES] = p[r, t]
        below = end + step
        if below < n:
            first, last = end // LANES, act[-1] + 1
            u = jnp.concatenate(
                [
                    jnp.concatenate([p[r, t] for t in range(first, last)], axis=1)
                    for r in range(r0, end, SUB)
                ],
                axis=0,
            )
            skip = below // LANES
            update = outer(u, (skip - first) * LANES, n - first * LANES)
            cut = slice(first * LANES, last * LANES)
            w[below:n, cut] = w[below:n, cut] - update[below - skip * LANES :, :]
        p = {at: value for at, value in p.items() if at[0] >= end}


def pack(r, out):
    n = r.shape[0]
    q = n // 4
    out[:q, :] = r[:q, :]
    out[q : 2 * q, :] = r[q : 2 * q, :]
    out[q : 2 * q, :q] = r[3 * q :, 3 * q :]
    out[2 * q :, : 2 * q] = r[2 * q : 2 * q + q // 2, 2 * q :]
    out[2 * q :, 2 * q :] = r[2 * q + q // 2 : 3 * q, 2 * q :]


def unpack(packed, r):
    n = r.shape[0]
    q = n // 4
    r[:q, :] = packed[:q, :]
    r[q : 2 * q, :] = packed[q : 2 * q, :]
    r[q : 2 * q, :q] = jnp.zeros((q, q), r.dtype)
    r[2 * q :, : 2 * q] = jnp.zeros((2 * q, 2 * q), r.dtype)
    r[2 * q : 2 * q + q // 2, 2 * q :] = packed[2 * q :, : 2 * q]
    r[2 * q + q // 2 : 3 * q, 2 * q :] = packed[2 * q :, 2 * q :]
    r[3 * q :, 2 * q : 3 * q] = jnp.zeros((q, q), r.dtype)
    r[3 * q :, 3 * q :] = packed[q : 2 * q, :q]


def sender_allows(compat, r, each, rows):
    sender = lax.axis_index("blk") ^ r
    return compat[0, sender * each // (rows // compat.shape[1])].astype(jnp.float32)


def product_t(x, y):
    return lax.dot_general(x, y, (((0,), (0,)), ((), ())), preferred_element_type=jnp.float32)


def gram_of(rounds, rows, compat, blocks, others=None):
    total = None
    for r, block, other in zip(rounds, blocks, blocks if others is None else others):
        part = product_t(block[...], other[...]) * sender_allows(compat, r, block.shape[0], rows)
        total = part if total is None else total + part
    return total


def gram_part(rounds, rows, compat, *refs):
    refs[-1][...] = gram_of(rounds, rows, compat, refs[:-1])


def shifted(g, size, row, col):
    i = lax.broadcasted_iota(jnp.int32, g.shape, 0) + row
    j = lax.broadcasted_iota(jnp.int32, g.shape, 1) + col
    live = jnp.logical_and(i < size[0, 0], j < size[0, 0])
    return jnp.where(live, (1.0 + SHIFT) * g, 0.0) + jnp.where(i == j, SHIFT * SHIFT, 0.0)


def factor_block(a, r_out, inverse_out, w):
    n = a.shape[0]
    i = lax.broadcasted_iota(jnp.int32, (n, n), 0)
    j = lax.broadcasted_iota(jnp.int32, (n, n), 1)
    w[:, :n] = a
    w[:, n:] = (i == j).astype(jnp.float32)
    factor_in_place(w, n)
    r_out[...] = jnp.where(i <= j, w[:, :n], 0.0)
    inverse_out[...] = jnp.where(i >= j, w[:, n:], 0.0)


def leading_factor(rounds, rows, compat, size, gram, *refs):
    *blocks, r_out, inverse_out, w = refs
    h = r_out.shape[0]
    g = gram[:h, :h] + gram_of(rounds, rows, compat, blocks)
    factor_block(shifted(g, size, 0, 0), r_out, inverse_out, w)


def trailing_factor(rounds, rows, compat, size, gram, r_lead, inverse_lead, *refs):
    *blocks, r_out, packed_out, inverse_out, w = refs
    first, second = blocks[: len(rounds)], blocks[len(rounds) :]
    h = r_lead.shape[0]
    cross = shifted(gram[:h, h:] + gram_of(rounds, rows, compat, first, second), size, 0, h)
    own = shifted(gram[h:, h:] + gram_of(rounds, rows, compat, second), size, h, h)
    dot = functools.partial(jnp.dot, preferred_element_type=jnp.float32)
    right = dot(inverse_lead[...], cross, precision=HIGHEST)
    down_t = functools.partial(
        lax.dot_general,
        dimension_numbers=(((0,), (0,)), ((), ())),
        precision=HIGHEST,
        preferred_element_type=jnp.float32,
    )
    right = right + dot(inverse_lead[...], cross - down_t(r_lead[...], right))
    factor_block(own - down_t(right, right), r_out.at[h:, h:], inverse_out, w)
    r_out[:h, :h] = r_lead[...]
    r_out[:h, h:] = right
    r_out[h:, :h] = jnp.zeros((h, h), jnp.float32)
    pack(r_out, packed_out)


def orthonormal_rows(rounds, rows, compat, size, factor, lead, trail, *refs):
    *blocks, out, results, sent = refs
    dims = (((1,), (1,)), ((), ()))
    h = lead.shape[0]
    below = lax.dot_general(
        factor[:h, h:],
        lead[...],
        (((0,), (0,)), ((), ())),
        precision=HIGHEST,
        preferred_element_type=jnp.float32,
    )
    below = -jnp.dot(trail[...], below, precision=HIGHEST, preferred_element_type=jnp.float32)
    inverse = jnp.concatenate(
        [
            jnp.concatenate([lead[...], jnp.zeros((h, h), jnp.float32)], axis=1),
            jnp.concatenate([below, trail[...]], axis=1),
        ],
        axis=0,
    )
    inverse = jnp.where(lax.broadcasted_iota(jnp.int32, inverse.shape, 1) < size[0, 0], inverse, 0.0)
    high = inverse.astype(jnp.bfloat16)
    low = (inverse - high.astype(jnp.float32)).astype(jnp.bfloat16)
    each = results.shape[1]
    me = lax.axis_index("blk")
    copies = []
    views = iter(blocks)
    for i, (r, pieces) in enumerate(rounds):
        x = jnp.concatenate([next(views)[...] for _ in range(pieces)], axis=1)
        q = lax.dot_general(x, high, dims, preferred_element_type=jnp.float32)
        q = q + lax.dot_general(x, low, dims, preferred_element_type=jnp.float32)
        results[i] = (q * sender_allows(compat, r, each, rows)).astype(jnp.bfloat16)
        place = pl.ds(pl.multiple_of((me ^ r) * each, each), each)
        copies.append(pltpu.make_async_copy(results.at[i], out.at[0, place], sent.at[i]))
        copies[-1].start()
    for copy in copies:
        copy.wait()


def chained(by, own, incoming, out, *rest):
    *packed_out, before = rest
    later = lax.axis_index("seg") >= by

    @pl.when(later)
    def _():
        unpack(incoming, before)
        h = own.shape[0] // 2
        dot = functools.partial(jnp.dot, precision=HIGHEST, preferred_element_type=jnp.float32)
        out[:h, :] = dot(own[:h, :], before[...])
        out[h:, :h] = jnp.zeros((h, h), jnp.float32)
        out[h:, h:] = dot(own[h:, h:], before[h:, h:])

    @pl.when(jnp.logical_not(later))
    def _():
        out[...] = own[...]

    for packed in packed_out:
        pack(out, packed)


def local(products, compat, sizes):
    parts = lax.axis_size("blk")
    rows_here, width = products.shape[1], products.shape[2] // parts
    rows = rows_here * parts
    f32 = functools.partial(jax.ShapeDtypeStruct, dtype=jnp.float32)
    b16 = functools.partial(jax.ShapeDtypeStruct, dtype=jnp.bfloat16)
    in_smem = pl.BlockSpec(memory_space=pltpu.SMEM)
    in_vmem = pl.BlockSpec(memory_space=pltpu.VMEM)
    in_hbm = pl.BlockSpec(memory_space=pltpu.MemorySpace.HBM)
    pieces = 4
    far, near = range(parts // 2, parts), range(1, parts // 2)
    whole, late = far[:-LATE], far[-LATE:]
    h = width // 2
    first, second = [(r, 0, h) for r in late], [(r, h, h) for r in late]
    far_sends = [(r, 0, width) for r in whole]
    cut = len(far_sends) - AHEAD
    far_sends = far_sends[:cut] + first + far_sends[cut:] + second
    near_sends = [(r, 0, width) for r in near]
    wanted = [(0, 0, width)] + far_sends + near_sends
    blocks = pl.pallas_call(
        functools.partial(split_columns, wanted),
        out_shape=[b16((rows_here, count)) for _, _, count in wanted],
        in_specs=[in_hbm],
        out_specs=[in_vmem] * len(wanted),
        scratch_shapes=[
            pltpu.VMEM((rows_here, parts * width), jnp.bfloat16),
            pltpu.SemaphoreType.DMA((pieces,)),
        ],
        compiler_params=PARAMS,
    )(products)
    blocks = dict(zip(wanted, blocks))
    got = {wanted[0]: blocks[wanted[0]]}
    for order, window in ((far_sends, FAR), (near_sends, NEAR)):
        for i, key in enumerate(order):
            block = blocks[key]
            if i >= window:
                block, _ = lax.optimization_barrier((block, got[order[i - window]]))
            got[key] = lax.ppermute(block, "blk", [(k, k ^ key[0]) for k in range(parts)])
    early = [0, *near, *whole]
    gram = pl.pallas_call(
        functools.partial(gram_part, early, rows),
        out_shape=f32((width, width)),
        in_specs=[in_smem] + [in_vmem] * len(early),
        out_specs=in_vmem,
        compiler_params=PARAMS,
    )(compat[0], *[got[r, 0, width] for r in early])
    firsts, seconds = [got[key] for key in first], [got[key] for key in second]
    lead_r, lead = pl.pallas_call(
        functools.partial(leading_factor, late, rows),
        out_shape=(f32((h, h)), f32((h, h))),
        in_specs=[in_smem, in_smem] + [in_vmem] * (1 + LATE),
        out_specs=[in_vmem] * 2,
        scratch_shapes=[pltpu.VMEM((h, 2 * h), jnp.float32)],
        compiler_params=PARAMS,
    )(compat[0], sizes, gram, *firsts)
    packed_rows = 5 * width // 8
    factor, packed, trail = pl.pallas_call(
        functools.partial(trailing_factor, late, rows),
        out_shape=(f32((width, width)), f32((packed_rows, width)), f32((h, h))),
        in_specs=[in_smem, in_smem] + [in_vmem] * (3 + 2 * LATE),
        out_specs=[in_vmem] * 3,
        scratch_shapes=[pltpu.VMEM((h, 2 * h), jnp.float32)],
        compiler_params=PARAMS,
    )(compat[0], sizes, gram, lead_r, lead, *firsts, *seconds)
    rounds = [(r, 1) for r in early] + [(r, 2) for r in late]
    views = [got[r, 0, width] for r in early] + [x for pair in zip(firsts, seconds) for x in pair]
    ortho = pl.pallas_call(
        functools.partial(orthonormal_rows, rounds, rows),
        out_shape=b16((1, rows, width)),
        in_specs=[in_smem, in_smem] + [in_vmem] * (3 + len(views)),
        out_specs=in_hbm,
        scratch_shapes=[
            pltpu.VMEM((parts, rows_here, width), jnp.bfloat16),
            pltpu.SemaphoreType.DMA((parts,)),
        ],
        compiler_params=PARAMS,
        cost_estimate=pl.CostEstimate(
            flops=4 * rows * width * width, bytes_accessed=4 * rows * width, transcendentals=0
        ),
    )(compat[0], sizes, factor, lead, trail, *views)
    sites = lax.axis_size("seg")
    accumulated, by = factor, 1
    while by < sites:
        incoming = lax.ppermute(packed, "seg", [(i, (i + by) % sites) for i in range(sites)])
        shapes = [f32((width, width)), f32((packed_rows, width))][: 1 if by * 2 >= sites else 2]
        accumulated, *packed = pl.pallas_call(
            functools.partial(chained, by),
            out_shape=shapes,
            in_specs=[in_vmem] * 2,
            out_specs=[in_vmem] * len(shapes),
            scratch_shapes=[pltpu.VMEM((width, width), jnp.float32)],
            compiler_params=PARAMS,
        )(accumulated, incoming)
        packed = packed[0] if packed else None
        by *= 2
    return (ortho, accumulated[None, None])


def solution(mesh):
    in_specs = (P("seg", "blk", None), P("seg", "blk", None), P("seg", "blk"))
    out_specs = (P("seg", None, "blk"), P("seg", "blk", None, None))
    return jax.shard_map(local, mesh=mesh, in_specs=in_specs, out_specs=out_specs, check_vma=False)
```

```python
import functools

import jax
import jax.numpy as jnp
from jax import lax
from jax.experimental import pallas as pl
from jax.experimental.pallas import tpu as pltpu
from jax.sharding import PartitionSpec as P

SHIFT = 0.05
HIGHEST = lax.Precision.HIGHEST
PARAMS = pltpu.CompilerParams(vmem_limit_bytes=48 << 20)
LANES = 128
SUB = 8
FAR, NEAR, LATE, AHEAD = 5, 3, 3, 3


def down(x, c):
    return jnp.broadcast_to(x[c : c + 1, :], (SUB, LANES))


def across(x, c):
    return jnp.broadcast_to(x[:, c : c + 1], (SUB, LANES))


def split_columns(wanted, src, *refs):
    *outs, rows, arrived = refs
    total = rows.shape[0]
    parts = arrived.shape[0]
    each = total // parts
    width = rows.shape[1] // lax.axis_size("blk")
    me = lax.axis_index("blk")
    cuts = [pl.ds(i * each, each) for i in range(parts)]
    reads = [pltpu.make_async_copy(src.at[0, cut], rows.at[cut], arrived.at[i]) for i, cut in enumerate(cuts)]
    for read in reads:
        read.start()
    for cut, read in zip(cuts, reads):
        read.wait()
        for (r, first, count), out in zip(wanted, outs):
            at = pl.multiple_of((me ^ r) * width + first, LANES)
            out[cut, :] = rows[cut, pl.ds(at, count)]


def outer(u, first, last):
    high = u.astype(jnp.bfloat16)
    rest = u - high.astype(jnp.float32)
    mid = rest.astype(jnp.bfloat16)
    low = (rest - mid.astype(jnp.float32)).astype(jnp.bfloat16)
    left = jnp.concatenate([x[:, first:last] for x in (high, high, mid, high, mid, low)], axis=0)
    right = jnp.concatenate([high, mid, high, low, mid, high], axis=0)
    return lax.dot_general(left, right, (((0,), (0,)), ((), ())), preferred_element_type=jnp.float32)


def factor_in_place(w, n, step=16):
    row_at = lax.broadcasted_iota(jnp.int32, (SUB, LANES), 0)
    lanes = 2 * n // LANES
    p = {}
    for r0 in range(0, n, step):
        half, base = r0 // LANES, r0 % LANES
        end = r0 + step
        act = range(half, min(lanes, half + n // LANES + 1))
        held = range(r0, min(end + step, n), SUB)
        for r in held:
            for t in act:
                if (r, t) not in p:
                    p[r, t] = w[r : r + SUB, t * LANES : (t + 1) * LANES]
        cols = {}
        for r in held:
            for c in range(min(step, r - r0 + SUB)):
                cols[r, c] = across(p[r, half], base + c)
        pivots = {r: jnp.ones((SUB, LANES), jnp.float32) for r in range(r0, end, SUB)}
        for c in range(step):
            own, at = r0 + c // SUB * SUB, c % SUB
            pivot = jnp.maximum(down(cols[own, c], at), SHIFT * SHIFT)
            inverse = 1.0 / pivot
            pivots[own] = jnp.where(row_at == at, pivot, pivots[own])
            row = {t: down(p[own, t], at) for t in act}
            ahead = {d: down(cols[r0 + d // SUB * SUB, c], d % SUB) for d in range(c + 1, step)}
            for r in held:
                if r < own or (r == own and at == SUB - 1):
                    continue
                x = cols[r, c]
                if r == own:
                    x = jnp.where(row_at > at, x, 0.0)
                times = x * inverse
                for d in range(c + 1, step):
                    if (r, d) not in cols:
                        continue
                    if d == c + 1 and r == r0 + d // SUB * SUB:
                        cols[r, d] = cols[r, d] - (x * ahead[d]) * inverse
                    else:
                        cols[r, d] = cols[r, d] - times * ahead[d]
                for t in act:
                    p[r, t] = p[r, t] - times * row[t]
        for r in range(r0, end, SUB):
            scale = lax.rsqrt(pivots[r])
            for t in act:
                p[r, t] = p[r, t] * scale
                w[r : r + SUB, t * LANES : (t + 1) * LANES] = p[r, t]
        below = end + step
        if below < n:
            first, last = end // LANES, act[-1] + 1
            u = jnp.concatenate(
                [
                    jnp.concatenate([p[r, t] for t in range(first, last)], axis=1)
                    for r in range(r0, end, SUB)
                ],
                axis=0,
            )
            skip = below // LANES
            update = outer(u, (skip - first) * LANES, n - first * LANES)
            cut = slice(first * LANES, last * LANES)
            w[below:n, cut] = w[below:n, cut] - update[below - skip * LANES :, :]
        p = {at: value for at, value in p.items() if at[0] >= end}


def sender_allows(compat, r, each, rows):
    sender = lax.axis_index("blk") ^ r
    return compat[0, sender * each // (rows // compat.shape[1])].astype(jnp.float32)


def product_t(x, y):
    return lax.dot_general(x, y, (((0,), (0,)), ((), ())), preferred_element_type=jnp.float32)


def gram_of(rounds, rows, compat, blocks, others=None):
    total = None
    for r, block, other in zip(rounds, blocks, blocks if others is None else others):
        part = product_t(block[...], other[...]) * sender_allows(compat, r, block.shape[0], rows)
        total = part if total is None else total + part
    return total


def gram_part(rounds, rows, compat, *refs):
    refs[-1][...] = gram_of(rounds, rows, compat, refs[:-1])


def shifted(g, size, row, col):
    i = lax.broadcasted_iota(jnp.int32, g.shape, 0) + row
    j = lax.broadcasted_iota(jnp.int32, g.shape, 1) + col
    live = jnp.logical_and(i < size[0, 0], j < size[0, 0])
    return jnp.where(live, (1.0 + SHIFT) * g, 0.0) + jnp.where(i == j, SHIFT * SHIFT, 0.0)


def factor_block(a, r_out, inverse_out, w):
    n = a.shape[0]
    i = lax.broadcasted_iota(jnp.int32, (n, n), 0)
    j = lax.broadcasted_iota(jnp.int32, (n, n), 1)
    w[:, :n] = a
    w[:, n:] = (i == j).astype(jnp.float32)
    factor_in_place(w, n)
    r_out[...] = jnp.where(i <= j, w[:, :n], 0.0)
    inverse_out[...] = jnp.where(i >= j, w[:, n:], 0.0)


def leading_factor(rounds, rows, compat, size, gram, *refs):
    *blocks, r_out, inverse_out, w = refs
    h = r_out.shape[0]
    g = gram[:h, :h] + gram_of(rounds, rows, compat, blocks)
    factor_block(shifted(g, size, 0, 0), r_out, inverse_out, w)


def trailing_factor(rounds, rows, compat, size, gram, r_lead, inverse_lead, *refs):
    *blocks, r_out, rest_out, inverse_out, w = refs
    first, second = blocks[: len(rounds)], blocks[len(rounds) :]
    h = r_lead.shape[0]
    cross = shifted(gram[:h, h:] + gram_of(rounds, rows, compat, first, second), size, 0, h)
    own = shifted(gram[h:, h:] + gram_of(rounds, rows, compat, second), size, h, h)
    dot = functools.partial(jnp.dot, preferred_element_type=jnp.float32)
    right = dot(inverse_lead[...], cross, precision=HIGHEST)
    down_t = functools.partial(
        lax.dot_general,
        dimension_numbers=(((0,), (0,)), ((), ())),
        precision=HIGHEST,
        preferred_element_type=jnp.float32,
    )
    right = right + dot(inverse_lead[...], cross - down_t(r_lead[...], right))
    factor_block(own - down_t(right, right), rest_out.at[:, h:], inverse_out, w)
    rest_out[:, :h] = right
    r_out[:h, :h] = r_lead[...]
    r_out[:h, h:] = right
    r_out[h:, :h] = jnp.zeros((h, h), jnp.float32)
    r_out[h:, h:] = rest_out[:, h:]


def orthonormal_rows(rounds, rows, compat, size, factor, lead, trail, *refs):
    *blocks, out, results, sent = refs
    dims = (((1,), (1,)), ((), ()))
    h = lead.shape[0]
    below = lax.dot_general(
        factor[:h, h:],
        lead[...],
        (((0,), (0,)), ((), ())),
        precision=HIGHEST,
        preferred_element_type=jnp.float32,
    )
    below = -jnp.dot(trail[...], below, precision=HIGHEST, preferred_element_type=jnp.float32)
    inverse = jnp.concatenate(
        [
            jnp.concatenate([lead[...], jnp.zeros((h, h), jnp.float32)], axis=1),
            jnp.concatenate([below, trail[...]], axis=1),
        ],
        axis=0,
    )
    inverse = jnp.where(lax.broadcasted_iota(jnp.int32, inverse.shape, 1) < size[0, 0], inverse, 0.0)
    high = inverse.astype(jnp.bfloat16)
    low = (inverse - high.astype(jnp.float32)).astype(jnp.bfloat16)
    each = results.shape[1]
    me = lax.axis_index("blk")
    copies = []
    views = iter(blocks)
    for i, (r, pieces) in enumerate(rounds):
        x = jnp.concatenate([next(views)[...] for _ in range(pieces)], axis=1)
        q = lax.dot_general(x, high, dims, preferred_element_type=jnp.float32)
        q = q + lax.dot_general(x, low, dims, preferred_element_type=jnp.float32)
        results[i] = (q * sender_allows(compat, r, each, rows)).astype(jnp.bfloat16)
        place = pl.ds(pl.multiple_of((me ^ r) * each, each), each)
        copies.append(pltpu.make_async_copy(results.at[i], out.at[0, place], sent.at[i]))
        copies[-1].start()
    for copy in copies:
        copy.wait()


def chained(by, own, lead, rest, out, *parts_out):
    later = lax.axis_index("seg") >= by
    h = lead.shape[0]

    @pl.when(later)
    def _():
        dot = functools.partial(jnp.dot, precision=HIGHEST, preferred_element_type=jnp.float32)
        top = dot(own[:h, :h], jnp.concatenate([lead[...], rest[:, :h]], axis=1))
        right = dot(own[:, h:], rest[:, h:])
        out[:h, :h] = top[:, :h]
        out[:h, h:] = top[:, h:] + right[:h, :]
        out[h:, :h] = jnp.zeros((h, h), jnp.float32)
        out[h:, h:] = right[h:, :]

    @pl.when(jnp.logical_not(later))
    def _():
        out[...] = own[...]

    if parts_out:
        lead_out, rest_out = parts_out
        lead_out[...] = out[:h, :h]
        rest_out[:, :h] = out[:h, h:]
        rest_out[:, h:] = out[h:, h:]


def local(products, compat, sizes):
    parts = lax.axis_size("blk")
    rows_here, width = products.shape[1], products.shape[2] // parts
    rows = rows_here * parts
    f32 = functools.partial(jax.ShapeDtypeStruct, dtype=jnp.float32)
    b16 = functools.partial(jax.ShapeDtypeStruct, dtype=jnp.bfloat16)
    in_smem = pl.BlockSpec(memory_space=pltpu.SMEM)
    in_vmem = pl.BlockSpec(memory_space=pltpu.VMEM)
    in_hbm = pl.BlockSpec(memory_space=pltpu.MemorySpace.HBM)
    pieces = 4
    far, near = range(parts // 2, parts), range(1, parts // 2)
    whole, late = far[:-LATE], far[-LATE:]
    h = width // 2
    first, second = [(r, 0, h) for r in late], [(r, h, h) for r in late]
    far_sends = [(r, 0, width) for r in whole]
    cut = len(far_sends) - AHEAD
    far_sends = far_sends[:cut] + first + far_sends[cut:] + second
    near_sends = [(r, 0, width) for r in near]
    wanted = [(0, 0, width)] + far_sends + near_sends
    blocks = pl.pallas_call(
        functools.partial(split_columns, wanted),
        out_shape=[b16((rows_here, count)) for _, _, count in wanted],
        in_specs=[in_hbm],
        out_specs=[in_vmem] * len(wanted),
        scratch_shapes=[
            pltpu.VMEM((rows_here, parts * width), jnp.bfloat16),
            pltpu.SemaphoreType.DMA((pieces,)),
        ],
        compiler_params=PARAMS,
    )(products)
    blocks = dict(zip(wanted, blocks))
    got = {wanted[0]: blocks[wanted[0]]}
    for order, window in ((far_sends, FAR), (near_sends, NEAR)):
        for i, key in enumerate(order):
            block = blocks[key]
            if i >= window:
                block, _ = lax.optimization_barrier((block, got[order[i - window]]))
            got[key] = lax.ppermute(block, "blk", [(k, k ^ key[0]) for k in range(parts)])
    early = [0, *near, *whole]
    gram = pl.pallas_call(
        functools.partial(gram_part, early, rows),
        out_shape=f32((width, width)),
        in_specs=[in_smem] + [in_vmem] * len(early),
        out_specs=in_vmem,
        compiler_params=PARAMS,
    )(compat[0], *[got[r, 0, width] for r in early])
    firsts, seconds = [got[key] for key in first], [got[key] for key in second]
    lead_r, lead = pl.pallas_call(
        functools.partial(leading_factor, late, rows),
        out_shape=(f32((h, h)), f32((h, h))),
        in_specs=[in_smem, in_smem] + [in_vmem] * (1 + LATE),
        out_specs=[in_vmem] * 2,
        scratch_shapes=[pltpu.VMEM((h, 2 * h), jnp.float32)],
        compiler_params=PARAMS,
    )(compat[0], sizes, gram, *firsts)
    sites = lax.axis_size("seg")

    def onward(x, by):
        return lax.ppermute(x, "seg", [(i, (i + by) % sites) for i in range(sites)])

    lead_in = onward(lead_r, 1)
    factor, rest, trail = pl.pallas_call(
        functools.partial(trailing_factor, late, rows),
        out_shape=(f32((width, width)), f32((h, width)), f32((h, h))),
        in_specs=[in_smem, in_smem] + [in_vmem] * (3 + 2 * LATE),
        out_specs=[in_vmem] * 3,
        scratch_shapes=[pltpu.VMEM((h, 2 * h), jnp.float32)],
        compiler_params=PARAMS,
    )(compat[0], sizes, gram, lead_r, lead, *firsts, *seconds)
    rounds = [(r, 1) for r in early] + [(r, 2) for r in late]
    views = [got[r, 0, width] for r in early] + [x for pair in zip(firsts, seconds) for x in pair]
    ortho = pl.pallas_call(
        functools.partial(orthonormal_rows, rounds, rows),
        out_shape=b16((1, rows, width)),
        in_specs=[in_smem, in_smem] + [in_vmem] * (3 + len(views)),
        out_specs=in_hbm,
        scratch_shapes=[
            pltpu.VMEM((parts, rows_here, width), jnp.bfloat16),
            pltpu.SemaphoreType.DMA((parts,)),
        ],
        compiler_params=PARAMS,
        cost_estimate=pl.CostEstimate(
            flops=4 * rows * width * width, bytes_accessed=4 * rows * width, transcendentals=0
        ),
    )(compat[0], sizes, factor, lead, trail, *views)
    accumulated, by = factor, 1
    while by < sites:
        rest, lead_in = lax.optimization_barrier((rest, lead_in))
        rest_in = onward(rest, by)
        shapes = [f32((width, width)), f32((h, h)), f32((h, width))][: 1 if by * 2 >= sites else 3]
        accumulated, *others = pl.pallas_call(
            functools.partial(chained, by),
            out_shape=shapes,
            in_specs=[in_vmem] * 3,
            out_specs=[in_vmem] * len(shapes),
            compiler_params=PARAMS,
        )(accumulated, lead_in, rest_in)
        by *= 2
        if others:
            lead_in, rest = onward(others[0], by), others[1]
    return (ortho, accumulated[None, None])


def solution(mesh):
    in_specs = (P("seg", "blk", None), P("seg", "blk", None), P("seg", "blk"))
    out_specs = (P("seg", None, "blk"), P("seg", "blk", None, None))
    return jax.shard_map(local, mesh=mesh, in_specs=in_specs, out_specs=out_specs, check_vma=False)
```

```python
import functools

import jax
import jax.numpy as jnp
from jax import lax
from jax.experimental import pallas as pl
from jax.experimental.pallas import tpu as pltpu
from jax.sharding import PartitionSpec as P

SHIFT = 0.05
HIGHEST = lax.Precision.HIGHEST
PARAMS = pltpu.CompilerParams(vmem_limit_bytes=48 << 20)
LANES = 128
SUB = 8
FAR, NEAR, LATE, AHEAD = 5, 3, 3, 3


def down(x, c):
    return jnp.broadcast_to(x[c : c + 1, :], (SUB, LANES))


def across(x, c):
    return jnp.broadcast_to(x[:, c : c + 1], (SUB, LANES))


def split_columns(wanted, src, *refs):
    *outs, rows, arrived = refs
    total = rows.shape[0]
    parts = arrived.shape[0]
    each = total // parts
    width = rows.shape[1] // lax.axis_size("blk")
    me = lax.axis_index("blk")
    cuts = [pl.ds(i * each, each) for i in range(parts)]
    reads = [pltpu.make_async_copy(src.at[0, cut], rows.at[cut], arrived.at[i]) for i, cut in enumerate(cuts)]
    for read in reads:
        read.start()
    for cut, read in zip(cuts, reads):
        read.wait()
        for (r, first, count), out in zip(wanted, outs):
            at = pl.multiple_of((me ^ r) * width + first, LANES)
            out[cut, :] = rows[cut, pl.ds(at, count)]


def outer(u, first, last):
    high = u.astype(jnp.bfloat16)
    rest = u - high.astype(jnp.float32)
    mid = rest.astype(jnp.bfloat16)
    low = (rest - mid.astype(jnp.float32)).astype(jnp.bfloat16)
    left = jnp.concatenate([x[:, first:last] for x in (high, high, mid, high, mid, low)], axis=0)
    right = jnp.concatenate([high, mid, high, low, mid, high], axis=0)
    return lax.dot_general(left, right, (((0,), (0,)), ((), ())), preferred_element_type=jnp.float32)


def factor_in_place(w, n, step=16):
    row_at = lax.broadcasted_iota(jnp.int32, (SUB, LANES), 0)
    lanes = 2 * n // LANES
    p = {}
    for r0 in range(0, n, step):
        half, base = r0 // LANES, r0 % LANES
        end = r0 + step
        act = range(half, min(lanes, half + n // LANES + 1))
        held = range(r0, min(end + step, n), SUB)
        for r in held:
            for t in act:
                if (r, t) not in p:
                    p[r, t] = w[r : r + SUB, t * LANES : (t + 1) * LANES]
        cols = {}
        for r in held:
            for c in range(min(step, r - r0 + SUB)):
                cols[r, c] = across(p[r, half], base + c)
        pivots = {r: jnp.ones((SUB, LANES), jnp.float32) for r in range(r0, end, SUB)}
        for c in range(step):
            own, at = r0 + c // SUB * SUB, c % SUB
            pivot = jnp.maximum(down(cols[own, c], at), SHIFT * SHIFT)
            inverse = 1.0 / pivot
            pivots[own] = jnp.where(row_at == at, pivot, pivots[own])
            row = {t: down(p[own, t], at) for t in act}
            ahead = {d: down(cols[r0 + d // SUB * SUB, c], d % SUB) for d in range(c + 1, step)}
            for r in held:
                if r < own or (r == own and at == SUB - 1):
                    continue
                x = cols[r, c]
                if r == own:
                    x = jnp.where(row_at > at, x, 0.0)
                times = x * inverse
                for d in range(c + 1, step):
                    if (r, d) not in cols:
                        continue
                    if d == c + 1 and r == r0 + d // SUB * SUB:
                        cols[r, d] = cols[r, d] - (x * ahead[d]) * inverse
                    else:
                        cols[r, d] = cols[r, d] - times * ahead[d]
                for t in act:
                    p[r, t] = p[r, t] - times * row[t]
        for r in range(r0, end, SUB):
            scale = lax.rsqrt(pivots[r])
            for t in act:
                p[r, t] = p[r, t] * scale
                w[r : r + SUB, t * LANES : (t + 1) * LANES] = p[r, t]
        below = end + step
        if below < n:
            first, last = end // LANES, act[-1] + 1
            u = jnp.concatenate(
                [
                    jnp.concatenate([p[r, t] for t in range(first, last)], axis=1)
                    for r in range(r0, end, SUB)
                ],
                axis=0,
            )
            skip = below // LANES
            update = outer(u, (skip - first) * LANES, n - first * LANES)
            cut = slice(first * LANES, last * LANES)
            w[below:n, cut] = w[below:n, cut] - update[below - skip * LANES :, :]
        p = {at: value for at, value in p.items() if at[0] >= end}


def sender_allows(compat, r, each, rows):
    sender = lax.axis_index("blk") ^ r
    return compat[0, sender * each // (rows // compat.shape[1])].astype(jnp.float32)


def product_t(x, y):
    return lax.dot_general(x, y, (((0,), (0,)), ((), ())), preferred_element_type=jnp.float32)


def gram_of(rounds, rows, compat, blocks, others=None):
    total = None
    for r, block, other in zip(rounds, blocks, blocks if others is None else others):
        part = product_t(block[...], other[...]) * sender_allows(compat, r, block.shape[0], rows)
        total = part if total is None else total + part
    return total


def gram_part(rounds, rows, compat, *refs):
    refs[-1][...] = gram_of(rounds, rows, compat, refs[:-1])


def shifted(g, size, row, col):
    i = lax.broadcasted_iota(jnp.int32, g.shape, 0) + row
    j = lax.broadcasted_iota(jnp.int32, g.shape, 1) + col
    live = jnp.logical_and(i < size[0, 0], j < size[0, 0])
    return jnp.where(live, (1.0 + SHIFT) * g, 0.0) + jnp.where(i == j, SHIFT * SHIFT, 0.0)


def factor_block(a, r_out, inverse_out, w):
    n = a.shape[0]
    i = lax.broadcasted_iota(jnp.int32, (n, n), 0)
    j = lax.broadcasted_iota(jnp.int32, (n, n), 1)
    w[:, :n] = a
    w[:, n:] = (i == j).astype(jnp.float32)
    factor_in_place(w, n)
    r_out[...] = jnp.where(i <= j, w[:, :n], 0.0)
    inverse_out[...] = jnp.where(i >= j, w[:, n:], 0.0)


def leading_factor(rounds, rows, compat, size, gram, *refs):
    *blocks, r_out, inverse_out, w = refs
    h = r_out.shape[0]
    g = gram[:h, :h] + gram_of(rounds, rows, compat, blocks)
    factor_block(shifted(g, size, 0, 0), r_out, inverse_out, w)


def thrice(x, y):
    x_high, y_high = x.astype(jnp.bfloat16), y.astype(jnp.bfloat16)
    x_low = (x - x_high.astype(jnp.float32)).astype(jnp.bfloat16)
    y_low = (y - y_high.astype(jnp.float32)).astype(jnp.bfloat16)
    left = jnp.concatenate([x_high, x_high, x_low], axis=1)
    return jnp.dot(left, jnp.concatenate([y_high, y_low, y_high], axis=0), preferred_element_type=jnp.float32)


def trailing_factor(rounds, rows, compat, size, gram, r_lead, inverse_lead, *refs):
    *blocks, r_out, rest_out, inverse_out, w = refs
    first, second = blocks[: len(rounds)], blocks[len(rounds) :]
    h = r_lead.shape[0]
    cross = shifted(gram[:h, h:] + gram_of(rounds, rows, compat, first, second), size, 0, h)
    own = shifted(gram[h:, h:] + gram_of(rounds, rows, compat, second), size, h, h)
    dot = functools.partial(jnp.dot, preferred_element_type=jnp.float32)
    right = thrice(inverse_lead[...], cross)
    down_t = functools.partial(
        lax.dot_general,
        dimension_numbers=(((0,), (0,)), ((), ())),
        precision=HIGHEST,
        preferred_element_type=jnp.float32,
    )
    right = right + dot(inverse_lead[...], cross - down_t(r_lead[...], right))
    factor_block(own - down_t(right, right), rest_out.at[:, h:], inverse_out, w)
    rest_out[:, :h] = right
    r_out[:h, :h] = r_lead[...]
    r_out[:h, h:] = right
    r_out[h:, :h] = jnp.zeros((h, h), jnp.float32)
    r_out[h:, h:] = rest_out[:, h:]


def orthonormal_rows(rounds, rows, compat, size, factor, lead, trail, *refs):
    *blocks, out, results, sent = refs
    dims = (((1,), (1,)), ((), ()))
    h = lead.shape[0]
    below = lax.dot_general(
        factor[:h, h:],
        lead[...],
        (((0,), (0,)), ((), ())),
        precision=HIGHEST,
        preferred_element_type=jnp.float32,
    )
    below = -jnp.dot(trail[...], below, precision=HIGHEST, preferred_element_type=jnp.float32)
    inverse = jnp.concatenate(
        [
            jnp.concatenate([lead[...], jnp.zeros((h, h), jnp.float32)], axis=1),
            jnp.concatenate([below, trail[...]], axis=1),
        ],
        axis=0,
    )
    inverse = jnp.where(lax.broadcasted_iota(jnp.int32, inverse.shape, 1) < size[0, 0], inverse, 0.0)
    high = inverse.astype(jnp.bfloat16)
    low = (inverse - high.astype(jnp.float32)).astype(jnp.bfloat16)
    each = results.shape[1]
    me = lax.axis_index("blk")
    copies = []
    views = iter(blocks)
    for i, (r, pieces) in enumerate(rounds):
        x = jnp.concatenate([next(views)[...] for _ in range(pieces)], axis=1)
        q = lax.dot_general(x, high, dims, preferred_element_type=jnp.float32)
        q = q + lax.dot_general(x, low, dims, preferred_element_type=jnp.float32)
        results[i] = (q * sender_allows(compat, r, each, rows)).astype(jnp.bfloat16)
        place = pl.ds(pl.multiple_of((me ^ r) * each, each), each)
        copies.append(pltpu.make_async_copy(results.at[i], out.at[0, place], sent.at[i]))
        copies[-1].start()
    for copy in copies:
        copy.wait()


def chained(by, own, lead, rest, out, *parts_out):
    later = lax.axis_index("seg") >= by
    h = lead.shape[0]

    @pl.when(later)
    def _():
        top = thrice(own[:h, :h], jnp.concatenate([lead[...], rest[:, :h]], axis=1))
        right = thrice(own[:, h:], rest[:, h:])
        out[:h, :h] = top[:, :h]
        out[:h, h:] = top[:, h:] + right[:h, :]
        out[h:, :h] = jnp.zeros((h, h), jnp.float32)
        out[h:, h:] = right[h:, :]

    @pl.when(jnp.logical_not(later))
    def _():
        out[...] = own[...]

    if parts_out:
        lead_out, rest_out = parts_out
        lead_out[...] = out[:h, :h]
        rest_out[:, :h] = out[:h, h:]
        rest_out[:, h:] = out[h:, h:]


def local(products, compat, sizes):
    parts = lax.axis_size("blk")
    rows_here, width = products.shape[1], products.shape[2] // parts
    rows = rows_here * parts
    f32 = functools.partial(jax.ShapeDtypeStruct, dtype=jnp.float32)
    b16 = functools.partial(jax.ShapeDtypeStruct, dtype=jnp.bfloat16)
    in_smem = pl.BlockSpec(memory_space=pltpu.SMEM)
    in_vmem = pl.BlockSpec(memory_space=pltpu.VMEM)
    in_hbm = pl.BlockSpec(memory_space=pltpu.MemorySpace.HBM)
    pieces = 4
    far, near = range(parts // 2, parts), range(1, parts // 2)
    whole, late = far[:-LATE], far[-LATE:]
    h = width // 2
    first, second = [(r, 0, h) for r in late], [(r, h, h) for r in late]
    far_sends = [(r, 0, width) for r in whole]
    cut = len(far_sends) - AHEAD
    far_sends = far_sends[:cut] + first + far_sends[cut:] + second
    near_sends = [(r, 0, width) for r in near]
    wanted = [(0, 0, width)] + far_sends + near_sends
    blocks = pl.pallas_call(
        functools.partial(split_columns, wanted),
        out_shape=[b16((rows_here, count)) for _, _, count in wanted],
        in_specs=[in_hbm],
        out_specs=[in_vmem] * len(wanted),
        scratch_shapes=[
            pltpu.VMEM((rows_here, parts * width), jnp.bfloat16),
            pltpu.SemaphoreType.DMA((pieces,)),
        ],
        compiler_params=PARAMS,
    )(products)
    blocks = dict(zip(wanted, blocks))
    got = {wanted[0]: blocks[wanted[0]]}
    for order, window in ((far_sends, FAR), (near_sends, NEAR)):
        for i, key in enumerate(order):
            block = blocks[key]
            if i >= window:
                block, _ = lax.optimization_barrier((block, got[order[i - window]]))
            got[key] = lax.ppermute(block, "blk", [(k, k ^ key[0]) for k in range(parts)])
    early = [0, *near, *whole]
    gram = pl.pallas_call(
        functools.partial(gram_part, early, rows),
        out_shape=f32((width, width)),
        in_specs=[in_smem] + [in_vmem] * len(early),
        out_specs=in_vmem,
        cost_estimate=pl.CostEstimate(flops=2 * rows * width * width, bytes_accessed=2 * rows * width, transcendentals=0),
        compiler_params=PARAMS,
    )(compat[0], *[got[r, 0, width] for r in early])
    firsts, seconds = [got[key] for key in first], [got[key] for key in second]
    lead_r, lead = pl.pallas_call(
        functools.partial(leading_factor, late, rows),
        out_shape=(f32((h, h)), f32((h, h))),
        in_specs=[in_smem, in_smem] + [in_vmem] * (1 + LATE),
        out_specs=[in_vmem] * 2,
        scratch_shapes=[pltpu.VMEM((h, 2 * h), jnp.float32)],
        compiler_params=PARAMS,
    )(compat[0], sizes, gram, *firsts)
    sites = lax.axis_size("seg")

    def onward(x, by):
        return lax.ppermute(x, "seg", [(i, (i + by) % sites) for i in range(sites)])

    lead_in = onward(lead_r, 1)
    factor, rest, trail = pl.pallas_call(
        functools.partial(trailing_factor, late, rows),
        out_shape=(f32((width, width)), f32((h, width)), f32((h, h))),
        in_specs=[in_smem, in_smem] + [in_vmem] * (3 + 2 * LATE),
        out_specs=[in_vmem] * 3,
        scratch_shapes=[pltpu.VMEM((h, 2 * h), jnp.float32)],
        compiler_params=PARAMS,
    )(compat[0], sizes, gram, lead_r, lead, *firsts, *seconds)
    rounds = [(r, 1) for r in early] + [(r, 2) for r in late]
    views = [got[r, 0, width] for r in early] + [x for pair in zip(firsts, seconds) for x in pair]
    ortho = pl.pallas_call(
        functools.partial(orthonormal_rows, rounds, rows),
        out_shape=b16((1, rows, width)),
        in_specs=[in_smem, in_smem] + [in_vmem] * (3 + len(views)),
        out_specs=in_hbm,
        scratch_shapes=[
            pltpu.VMEM((parts, rows_here, width), jnp.bfloat16),
            pltpu.SemaphoreType.DMA((parts,)),
        ],
        compiler_params=PARAMS,
        cost_estimate=pl.CostEstimate(
            flops=4 * rows * width * width, bytes_accessed=4 * rows * width, transcendentals=0
        ),
    )(compat[0], sizes, factor, lead, trail, *views)
    accumulated, by = factor, 1
    while by < sites:
        rest, lead_in = lax.optimization_barrier((rest, lead_in))
        rest_in = onward(rest, by)
        shapes = [f32((width, width)), f32((h, h)), f32((h, width))][: 1 if by * 2 >= sites else 3]
        accumulated, *others = pl.pallas_call(
            functools.partial(chained, by),
            out_shape=shapes,
            in_specs=[in_vmem] * 3,
            out_specs=[in_vmem] * len(shapes),
            compiler_params=PARAMS,
        )(accumulated, lead_in, rest_in)
        by *= 2
        if others:
            lead_in, rest = onward(others[0], by), others[1]
    return (ortho, accumulated[None, None])


def solution(mesh):
    in_specs = (P("seg", "blk", None), P("seg", "blk", None), P("seg", "blk"))
    out_specs = (P("seg", None, "blk"), P("seg", "blk", None, None))
    return jax.shard_map(local, mesh=mesh, in_specs=in_specs, out_specs=out_specs, check_vma=False)
```

```python
import functools

import jax
import jax.numpy as jnp
from jax import lax
from jax.experimental import pallas as pl
from jax.experimental.pallas import tpu as pltpu
from jax.sharding import PartitionSpec as P

SHIFT = 0.05
HIGHEST = lax.Precision.HIGHEST
PARAMS = pltpu.CompilerParams(vmem_limit_bytes=48 << 20)
LANES = 128
SUB = 8
FAR, NEAR, LATE, AHEAD = 5, 3, 3, 3


def down(x, c):
    return jnp.broadcast_to(x[c : c + 1, :], (SUB, LANES))


def across(x, c):
    return jnp.broadcast_to(x[:, c : c + 1], (SUB, LANES))


def split_columns(wanted, src, *outs):
    width = src.shape[2] // lax.axis_size("blk")
    me = lax.axis_index("blk")
    for (r, first, count), out in zip(wanted, outs):
        at = pl.multiple_of((me ^ r) * width + first, LANES)
        out[...] = src[0, :, pl.ds(at, count)]


def outer(u, first, last):
    high = u.astype(jnp.bfloat16)
    rest = u - high.astype(jnp.float32)
    mid = rest.astype(jnp.bfloat16)
    low = (rest - mid.astype(jnp.float32)).astype(jnp.bfloat16)
    left = jnp.concatenate([x[:, first:last] for x in (high, high, mid, high, mid, low)], axis=0)
    right = jnp.concatenate([high, mid, high, low, mid, high], axis=0)
    return lax.dot_general(left, right, (((0,), (0,)), ((), ())), preferred_element_type=jnp.float32)


def factor_in_place(w, n, step=16):
    row_at = lax.broadcasted_iota(jnp.int32, (SUB, LANES), 0)
    lanes = 2 * n // LANES
    p = {}
    for r0 in range(0, n, step):
        half, base = r0 // LANES, r0 % LANES
        end = r0 + step
        act = range(half, min(lanes, half + n // LANES + 1))
        held = range(r0, min(end + step, n), SUB)
        for r in held:
            for t in act:
                if (r, t) not in p:
                    p[r, t] = w[r : r + SUB, t * LANES : (t + 1) * LANES]
        cols = {}
        for r in held:
            for c in range(min(step, r - r0 + SUB)):
                cols[r, c] = across(p[r, half], base + c)
        pivots = {r: jnp.ones((SUB, LANES), jnp.float32) for r in range(r0, end, SUB)}
        for c in range(step):
            own, at = r0 + c // SUB * SUB, c % SUB
            pivot = jnp.maximum(down(cols[own, c], at), SHIFT * SHIFT)
            inverse = 1.0 / pivot
            pivots[own] = jnp.where(row_at == at, pivot, pivots[own])
            row = {t: down(p[own, t], at) for t in act}
            ahead = {d: down(cols[r0 + d // SUB * SUB, c], d % SUB) for d in range(c + 1, step)}
            for r in held:
                if r < own or (r == own and at == SUB - 1):
                    continue
                x = cols[r, c]
                if r == own:
                    x = jnp.where(row_at > at, x, 0.0)
                times = x * inverse
                for d in range(c + 1, step):
                    if (r, d) not in cols:
                        continue
                    if d == c + 1 and r == r0 + d // SUB * SUB:
                        cols[r, d] = cols[r, d] - (x * ahead[d]) * inverse
                    else:
                        cols[r, d] = cols[r, d] - times * ahead[d]
                for t in act:
                    p[r, t] = p[r, t] - times * row[t]
        for r in range(r0, end, SUB):
            scale = lax.rsqrt(pivots[r])
            for t in act:
                p[r, t] = p[r, t] * scale
                w[r : r + SUB, t * LANES : (t + 1) * LANES] = p[r, t]
        below = end + step
        if below < n:
            first, last = end // LANES, act[-1] + 1
            u = jnp.concatenate(
                [
                    jnp.concatenate([p[r, t] for t in range(first, last)], axis=1)
                    for r in range(r0, end, SUB)
                ],
                axis=0,
            )
            skip = below // LANES
            update = outer(u, (skip - first) * LANES, n - first * LANES)
            cut = slice(first * LANES, last * LANES)
            w[below:n, cut] = w[below:n, cut] - update[below - skip * LANES :, :]
        p = {at: value for at, value in p.items() if at[0] >= end}


def sender_allows(compat, r, each, rows):
    sender = lax.axis_index("blk") ^ r
    return compat[0, sender * each // (rows // compat.shape[1])].astype(jnp.float32)


def product_t(x, y):
    return lax.dot_general(x, y, (((0,), (0,)), ((), ())), preferred_element_type=jnp.float32)


def gram_of(rounds, rows, compat, blocks, others=None):
    total = None
    for r, block, other in zip(rounds, blocks, blocks if others is None else others):
        part = product_t(block[...], other[...]) * sender_allows(compat, r, block.shape[0], rows)
        total = part if total is None else total + part
    return total


def gram_part(rounds, rows, compat, *refs):
    refs[-1][...] = gram_of(rounds, rows, compat, refs[:-1])


def shifted(g, size, row, col):
    i = lax.broadcasted_iota(jnp.int32, g.shape, 0) + row
    j = lax.broadcasted_iota(jnp.int32, g.shape, 1) + col
    live = jnp.logical_and(i < size[0, 0], j < size[0, 0])
    return jnp.where(live, (1.0 + SHIFT) * g, 0.0) + jnp.where(i == j, SHIFT * SHIFT, 0.0)


def factor_block(a, r_out, inverse_out, w):
    n = a.shape[0]
    i = lax.broadcasted_iota(jnp.int32, (n, n), 0)
    j = lax.broadcasted_iota(jnp.int32, (n, n), 1)
    w[:, :n] = a
    w[:, n:] = (i == j).astype(jnp.float32)
    factor_in_place(w, n)
    r_out[...] = jnp.where(i <= j, w[:, :n], 0.0)
    inverse_out[...] = jnp.where(i >= j, w[:, n:], 0.0)


def leading_factor(rounds, rows, compat, size, gram, *refs):
    *blocks, r_out, inverse_out, w = refs
    h = r_out.shape[0]
    g = gram[:h, :h] + gram_of(rounds, rows, compat, blocks)
    factor_block(shifted(g, size, 0, 0), r_out, inverse_out, w)


def thrice(x, y):
    x_high, y_high = x.astype(jnp.bfloat16), y.astype(jnp.bfloat16)
    x_low = (x - x_high.astype(jnp.float32)).astype(jnp.bfloat16)
    y_low = (y - y_high.astype(jnp.float32)).astype(jnp.bfloat16)
    left = jnp.concatenate([x_high, x_high, x_low], axis=1)
    return jnp.dot(left, jnp.concatenate([y_high, y_low, y_high], axis=0), preferred_element_type=jnp.float32)


def trailing_factor(rounds, rows, compat, size, gram, r_lead, inverse_lead, *refs):
    *blocks, r_out, rest_out, inverse_out, w = refs
    first, second = blocks[: len(rounds)], blocks[len(rounds) :]
    h = r_lead.shape[0]
    cross = shifted(gram[:h, h:] + gram_of(rounds, rows, compat, first, second), size, 0, h)
    own = shifted(gram[h:, h:] + gram_of(rounds, rows, compat, second), size, h, h)
    dot = functools.partial(jnp.dot, preferred_element_type=jnp.float32)
    right = thrice(inverse_lead[...], cross)
    down_t = functools.partial(
        lax.dot_general,
        dimension_numbers=(((0,), (0,)), ((), ())),
        precision=HIGHEST,
        preferred_element_type=jnp.float32,
    )
    right = right + dot(inverse_lead[...], cross - down_t(r_lead[...], right))
    factor_block(own - down_t(right, right), rest_out.at[:, h:], inverse_out, w)
    rest_out[:, :h] = right
    r_out[:h, :h] = r_lead[...]
    r_out[:h, h:] = right
    r_out[h:, :h] = jnp.zeros((h, h), jnp.float32)
    r_out[h:, h:] = rest_out[:, h:]


def orthonormal_rows(rounds, rows, compat, size, factor, lead, trail, *refs):
    *blocks, out, results, sent = refs
    dims = (((1,), (1,)), ((), ()))
    h = lead.shape[0]
    below = lax.dot_general(
        factor[:h, h:],
        lead[...],
        (((0,), (0,)), ((), ())),
        precision=HIGHEST,
        preferred_element_type=jnp.float32,
    )
    below = -jnp.dot(trail[...], below, precision=HIGHEST, preferred_element_type=jnp.float32)
    inverse = jnp.concatenate(
        [
            jnp.concatenate([lead[...], jnp.zeros((h, h), jnp.float32)], axis=1),
            jnp.concatenate([below, trail[...]], axis=1),
        ],
        axis=0,
    )
    inverse = jnp.where(lax.broadcasted_iota(jnp.int32, inverse.shape, 1) < size[0, 0], inverse, 0.0)
    high = inverse.astype(jnp.bfloat16)
    low = (inverse - high.astype(jnp.float32)).astype(jnp.bfloat16)
    each = results.shape[1]
    me = lax.axis_index("blk")
    copies = []
    views = iter(blocks)
    for i, (r, pieces) in enumerate(rounds):
        x = jnp.concatenate([next(views)[...] for _ in range(pieces)], axis=1)
        q = lax.dot_general(x, high, dims, preferred_element_type=jnp.float32)
        q = q + lax.dot_general(x, low, dims, preferred_element_type=jnp.float32)
        results[i] = (q * sender_allows(compat, r, each, rows)).astype(jnp.bfloat16)
        place = pl.ds(pl.multiple_of((me ^ r) * each, each), each)
        copies.append(pltpu.make_async_copy(results.at[i], out.at[0, place], sent.at[i]))
        copies[-1].start()
    for copy in copies:
        copy.wait()


def chained(by, own, lead, rest, out, *parts_out):
    later = lax.axis_index("seg") >= by
    h = lead.shape[0]

    @pl.when(later)
    def _():
        top = thrice(own[:h, :h], jnp.concatenate([lead[...], rest[:, :h]], axis=1))
        right = thrice(own[:, h:], rest[:, h:])
        out[:h, :h] = top[:, :h]
        out[:h, h:] = top[:, h:] + right[:h, :]
        out[h:, :h] = jnp.zeros((h, h), jnp.float32)
        out[h:, h:] = right[h:, :]

    @pl.when(jnp.logical_not(later))
    def _():
        out[...] = own[...]

    if parts_out:
        lead_out, rest_out = parts_out
        lead_out[...] = out[:h, :h]
        rest_out[:, :h] = out[:h, h:]
        rest_out[:, h:] = out[h:, h:]


def local(products, compat, sizes):
    parts = lax.axis_size("blk")
    rows_here, width = products.shape[1], products.shape[2] // parts
    rows = rows_here * parts
    f32 = functools.partial(jax.ShapeDtypeStruct, dtype=jnp.float32)
    b16 = functools.partial(jax.ShapeDtypeStruct, dtype=jnp.bfloat16)
    in_smem = pl.BlockSpec(memory_space=pltpu.SMEM)
    in_vmem = pl.BlockSpec(memory_space=pltpu.VMEM)
    in_hbm = pl.BlockSpec(memory_space=pltpu.MemorySpace.HBM)
    far, near = range(parts // 2, parts), range(1, parts // 2)
    whole, late = far[:-LATE], far[-LATE:]
    h = width // 2
    first, second = [(r, 0, h) for r in late], [(r, h, h) for r in late]
    far_sends = [(r, 0, width) for r in whole]
    cut = len(far_sends) - AHEAD
    far_sends = far_sends[:cut] + first + far_sends[cut:] + second
    near_sends = [(r, 0, width) for r in near]
    wanted = [(0, 0, width)] + far_sends + near_sends
    blocks = pl.pallas_call(
        functools.partial(split_columns, wanted),
        out_shape=[b16((rows_here, count)) for _, _, count in wanted],
        in_specs=[in_vmem],
        out_specs=[in_vmem] * len(wanted),
        compiler_params=PARAMS,
    )(products)
    blocks = dict(zip(wanted, blocks))
    got = {wanted[0]: blocks[wanted[0]]}
    for order, window in ((far_sends, FAR), (near_sends, NEAR)):
        for i, key in enumerate(order):
            block = blocks[key]
            if i >= window:
                block, _ = lax.optimization_barrier((block, got[order[i - window]]))
            got[key] = lax.ppermute(block, "blk", [(k, k ^ key[0]) for k in range(parts)])
    early = [0, *near, *whole]
    gram = pl.pallas_call(
        functools.partial(gram_part, early, rows),
        out_shape=f32((width, width)),
        in_specs=[in_smem] + [in_vmem] * len(early),
        out_specs=in_vmem,
        cost_estimate=pl.CostEstimate(flops=2 * rows * width * width, bytes_accessed=2 * rows * width, transcendentals=0),
        compiler_params=PARAMS,
    )(compat[0], *[got[r, 0, width] for r in early])
    firsts, seconds = [got[key] for key in first], [got[key] for key in second]
    lead_r, lead = pl.pallas_call(
        functools.partial(leading_factor, late, rows),
        out_shape=(f32((h, h)), f32((h, h))),
        in_specs=[in_smem, in_smem] + [in_vmem] * (1 + LATE),
        out_specs=[in_vmem] * 2,
        scratch_shapes=[pltpu.VMEM((h, 2 * h), jnp.float32)],
        compiler_params=PARAMS,
    )(compat[0], sizes, gram, *firsts)
    sites = lax.axis_size("seg")

    def onward(x, by):
        return lax.ppermute(x, "seg", [(i, (i + by) % sites) for i in range(sites)])

    lead_in = onward(lead_r, 1)
    factor, rest, trail = pl.pallas_call(
        functools.partial(trailing_factor, late, rows),
        out_shape=(f32((width, width)), f32((h, width)), f32((h, h))),
        in_specs=[in_smem, in_smem] + [in_vmem] * (3 + 2 * LATE),
        out_specs=[in_vmem] * 3,
        scratch_shapes=[pltpu.VMEM((h, 2 * h), jnp.float32)],
        compiler_params=PARAMS,
    )(compat[0], sizes, gram, lead_r, lead, *firsts, *seconds)
    rounds = [(r, 1) for r in early] + [(r, 2) for r in late]
    views = [got[r, 0, width] for r in early] + [x for pair in zip(firsts, seconds) for x in pair]
    ortho = pl.pallas_call(
        functools.partial(orthonormal_rows, rounds, rows),
        out_shape=b16((1, rows, width)),
        in_specs=[in_smem, in_smem] + [in_vmem] * (3 + len(views)),
        out_specs=in_hbm,
        scratch_shapes=[
            pltpu.VMEM((parts, rows_here, width), jnp.bfloat16),
            pltpu.SemaphoreType.DMA((parts,)),
        ],
        compiler_params=PARAMS,
        cost_estimate=pl.CostEstimate(
            flops=4 * rows * width * width, bytes_accessed=4 * rows * width, transcendentals=0
        ),
    )(compat[0], sizes, factor, lead, trail, *views)
    accumulated, by = factor, 1
    while by < sites:
        rest, lead_in = lax.optimization_barrier((rest, lead_in))
        rest_in = onward(rest, by)
        shapes = [f32((width, width)), f32((h, h)), f32((h, width))][: 1 if by * 2 >= sites else 3]
        accumulated, *others = pl.pallas_call(
            functools.partial(chained, by),
            out_shape=shapes,
            in_specs=[in_vmem] * 3,
            out_specs=[in_vmem] * len(shapes),
            compiler_params=PARAMS,
        )(accumulated, lead_in, rest_in)
        by *= 2
        if others:
            lead_in, rest = onward(others[0], by), others[1]
    return (ortho, accumulated[None, None])


def solution(mesh):
    in_specs = (P("seg", "blk", None), P("seg", "blk", None), P("seg", "blk"))
    out_specs = (P("seg", None, "blk"), P("seg", "blk", None, None))
    return jax.shard_map(local, mesh=mesh, in_specs=in_specs, out_specs=out_specs, check_vma=False)
```

```python
import functools

import jax
import jax.numpy as jnp
from jax import lax
from jax.experimental import pallas as pl
from jax.experimental.pallas import tpu as pltpu
from jax.sharding import PartitionSpec as P

SHIFT = 0.05
HIGHEST = lax.Precision.HIGHEST
PARAMS = pltpu.CompilerParams(vmem_limit_bytes=48 << 20)
LANES = 128
SUB = 8
FAR, NEAR, LATE, AHEAD = 5, 3, 3, 3


def down(x, c):
    return jnp.broadcast_to(x[c : c + 1, :], (SUB, LANES))


def across(x, c):
    return jnp.broadcast_to(x[:, c : c + 1], (SUB, LANES))


def split_columns(wanted, src, *outs):
    width = src.shape[2] // lax.axis_size("blk")
    me = lax.axis_index("blk")
    for (r, first, count), out in zip(wanted, outs):
        at = pl.multiple_of((me ^ r) * width + first, LANES)
        out[...] = src[0, :, pl.ds(at, count)]


def outer(u, first, last):
    high = u.astype(jnp.bfloat16)
    rest = u - high.astype(jnp.float32)
    mid = rest.astype(jnp.bfloat16)
    low = (rest - mid.astype(jnp.float32)).astype(jnp.bfloat16)
    left = jnp.concatenate([x[:, first:last] for x in (high, high, mid, high, mid, low)], axis=0)
    right = jnp.concatenate([high, mid, high, low, mid, high], axis=0)
    return lax.dot_general(left, right, (((0,), (0,)), ((), ())), preferred_element_type=jnp.float32)


def factor_in_place(w, n, step=16):
    row_at = lax.broadcasted_iota(jnp.int32, (SUB, LANES), 0)
    lanes = 2 * n // LANES
    p = {}
    for r0 in range(0, n, step):
        half, base = r0 // LANES, r0 % LANES
        end = r0 + step
        act = range(half, min(lanes, half + n // LANES + 1))
        held = range(r0, min(end + step, n), SUB)
        for r in held:
            for t in act:
                if (r, t) not in p:
                    p[r, t] = w[r : r + SUB, t * LANES : (t + 1) * LANES]
        cols = {}
        for r in held:
            for c in range(min(step, r - r0 + SUB)):
                cols[r, c] = across(p[r, half], base + c)
        pivots = {r: jnp.ones((SUB, LANES), jnp.float32) for r in range(r0, end, SUB)}
        for c in range(step):
            own, at = r0 + c // SUB * SUB, c % SUB
            pivot = jnp.maximum(down(cols[own, c], at), SHIFT * SHIFT)
            inverse = 1.0 / pivot
            pivots[own] = jnp.where(row_at == at, pivot, pivots[own])
            row = {t: down(p[own, t], at) for t in act}
            ahead = {d: down(cols[r0 + d // SUB * SUB, c], d % SUB) for d in range(c + 1, step)}
            for r in held:
                if r < own or (r == own and at == SUB - 1):
                    continue
                x = cols[r, c]
                if r == own:
                    x = jnp.where(row_at > at, x, 0.0)
                times = x * inverse
                for d in range(c + 1, step):
                    if (r, d) not in cols:
                        continue
                    if d == c + 1 and r == r0 + d // SUB * SUB:
                        cols[r, d] = cols[r, d] - (x * ahead[d]) * inverse
                    else:
                        cols[r, d] = cols[r, d] - times * ahead[d]
                for t in act:
                    p[r, t] = p[r, t] - times * row[t]
        for r in range(r0, end, SUB):
            scale = lax.rsqrt(pivots[r])
            for t in act:
                p[r, t] = p[r, t] * scale
                w[r : r + SUB, t * LANES : (t + 1) * LANES] = p[r, t]
        below = end + step
        if below < n:
            first, last = end // LANES, act[-1] + 1
            u = jnp.concatenate(
                [
                    jnp.concatenate([p[r, t] for t in range(first, last)], axis=1)
                    for r in range(r0, end, SUB)
                ],
                axis=0,
            )
            skip = below // LANES
            update = outer(u, (skip - first) * LANES, n - first * LANES)
            cut = slice(first * LANES, last * LANES)
            w[below:n, cut] = w[below:n, cut] - update[below - skip * LANES :, :]
        p = {at: value for at, value in p.items() if at[0] >= end}


def sender_allows(compat, r, each, rows):
    sender = lax.axis_index("blk") ^ r
    return compat[0, sender * each // (rows // compat.shape[1])].astype(jnp.float32)


def product_t(x, y):
    return lax.dot_general(x, y, (((0,), (0,)), ((), ())), preferred_element_type=jnp.float32)


def gram_of(rounds, rows, compat, blocks, others=None):
    total = None
    for r, block, other in zip(rounds, blocks, blocks if others is None else others):
        part = product_t(block[...], other[...]) * sender_allows(compat, r, block.shape[0], rows)
        total = part if total is None else total + part
    return total


def gram_part(rounds, rows, compat, *refs):
    refs[-1][...] = gram_of(rounds, rows, compat, refs[:-1])


def shifted(g, size, row, col):
    i = lax.broadcasted_iota(jnp.int32, g.shape, 0) + row
    j = lax.broadcasted_iota(jnp.int32, g.shape, 1) + col
    live = jnp.logical_and(i < size[0, 0], j < size[0, 0])
    return jnp.where(live, (1.0 + SHIFT) * g, 0.0) + jnp.where(i == j, SHIFT * SHIFT, 0.0)


def factor_block(a, r_out, inverse_out, w):
    n = a.shape[0]
    i = lax.broadcasted_iota(jnp.int32, (n, n), 0)
    j = lax.broadcasted_iota(jnp.int32, (n, n), 1)
    w[:, :n] = a
    w[:, n:] = (i == j).astype(jnp.float32)
    factor_in_place(w, n)
    r_out[...] = jnp.where(i <= j, w[:, :n], 0.0)
    inverse_out[...] = jnp.where(i >= j, w[:, n:], 0.0)


def leading_factor(rounds, rows, compat, size, gram, *refs):
    *blocks, r_out, lower_out, inverse_out, w = refs
    h = r_out.shape[0]
    g = gram[:h, :h] + gram_of(rounds, rows, compat, blocks)
    factor_block(shifted(g, size, 0, 0), r_out, inverse_out, w)
    lower_out[...] = r_out[...].T


def thrice(x, y):
    x_high, y_high = x.astype(jnp.bfloat16), y.astype(jnp.bfloat16)
    x_low = (x - x_high.astype(jnp.float32)).astype(jnp.bfloat16)
    y_low = (y - y_high.astype(jnp.float32)).astype(jnp.bfloat16)
    left = jnp.concatenate([x_high, x_high, x_low], axis=1)
    return jnp.dot(left, jnp.concatenate([y_high, y_low, y_high], axis=0), preferred_element_type=jnp.float32)


def trailing_factor(rounds, rows, compat, size, gram, r_lead, lower, inverse_lead, *refs):
    *blocks, r_out, rest_out, inverse_out, w = refs
    first, second = blocks[: len(rounds)], blocks[len(rounds) :]
    h = r_lead.shape[0]
    cross = shifted(gram[:h, h:] + gram_of(rounds, rows, compat, first, second), size, 0, h)
    own = shifted(gram[h:, h:] + gram_of(rounds, rows, compat, second), size, h, h)
    dot = functools.partial(jnp.dot, preferred_element_type=jnp.float32)
    right = thrice(inverse_lead[...], cross)
    down_t = functools.partial(
        lax.dot_general,
        dimension_numbers=(((0,), (0,)), ((), ())),
        precision=HIGHEST,
        preferred_element_type=jnp.float32,
    )
    right = right + dot(inverse_lead[...], cross - dot(lower[...], right, precision=HIGHEST))
    factor_block(own - down_t(right, right), rest_out.at[:, h:], inverse_out, w)
    rest_out[:, :h] = right
    r_out[:h, :h] = r_lead[...]
    r_out[:h, h:] = right
    r_out[h:, :h] = jnp.zeros((h, h), jnp.float32)
    r_out[h:, h:] = rest_out[:, h:]


def orthonormal_rows(rounds, rows, compat, size, factor, lead, trail, *refs):
    *blocks, out, results, sent = refs
    dims = (((1,), (1,)), ((), ()))
    h = lead.shape[0]
    below = lax.dot_general(
        factor[:h, h:],
        lead[...],
        (((0,), (0,)), ((), ())),
        precision=HIGHEST,
        preferred_element_type=jnp.float32,
    )
    below = -jnp.dot(trail[...], below, precision=HIGHEST, preferred_element_type=jnp.float32)
    inverse = jnp.concatenate(
        [
            jnp.concatenate([lead[...], jnp.zeros((h, h), jnp.float32)], axis=1),
            jnp.concatenate([below, trail[...]], axis=1),
        ],
        axis=0,
    )
    inverse = jnp.where(lax.broadcasted_iota(jnp.int32, inverse.shape, 1) < size[0, 0], inverse, 0.0)
    high = inverse.astype(jnp.bfloat16)
    low = (inverse - high.astype(jnp.float32)).astype(jnp.bfloat16)
    each = results.shape[1]
    me = lax.axis_index("blk")
    copies = []
    views = iter(blocks)
    for i, (r, pieces) in enumerate(rounds):
        x = jnp.concatenate([next(views)[...] for _ in range(pieces)], axis=1)
        q = lax.dot_general(x, high, dims, preferred_element_type=jnp.float32)
        q = q + lax.dot_general(x, low, dims, preferred_element_type=jnp.float32)
        results[i] = (q * sender_allows(compat, r, each, rows)).astype(jnp.bfloat16)
        place = pl.ds(pl.multiple_of((me ^ r) * each, each), each)
        copies.append(pltpu.make_async_copy(results.at[i], out.at[0, place], sent.at[i]))
        copies[-1].start()
    for copy in copies:
        copy.wait()


def chained(by, own, lead, rest, out, *parts_out):
    later = lax.axis_index("seg") >= by
    h = lead.shape[0]

    @pl.when(later)
    def _():
        top = thrice(own[:h, :h], jnp.concatenate([lead[...], rest[:, :h]], axis=1))
        right = thrice(own[:, h:], rest[:, h:])
        out[:h, :h] = top[:, :h]
        out[:h, h:] = top[:, h:] + right[:h, :]
        out[h:, :h] = jnp.zeros((h, h), jnp.float32)
        out[h:, h:] = right[h:, :]

    @pl.when(jnp.logical_not(later))
    def _():
        out[...] = own[...]

    if parts_out:
        lead_out, rest_out = parts_out
        lead_out[...] = out[:h, :h]
        rest_out[:, :h] = out[:h, h:]
        rest_out[:, h:] = out[h:, h:]


def local(products, compat, sizes):
    parts = lax.axis_size("blk")
    rows_here, width = products.shape[1], products.shape[2] // parts
    rows = rows_here * parts
    f32 = functools.partial(jax.ShapeDtypeStruct, dtype=jnp.float32)
    b16 = functools.partial(jax.ShapeDtypeStruct, dtype=jnp.bfloat16)
    in_smem = pl.BlockSpec(memory_space=pltpu.SMEM)
    in_vmem = pl.BlockSpec(memory_space=pltpu.VMEM)
    in_hbm = pl.BlockSpec(memory_space=pltpu.MemorySpace.HBM)
    far, near = range(parts // 2, parts), range(1, parts // 2)
    whole, late = far[:-LATE], far[-LATE:]
    h = width // 2
    first, second = [(r, 0, h) for r in late], [(r, h, h) for r in late]
    far_sends = [(r, 0, width) for r in whole]
    cut = len(far_sends) - AHEAD
    far_sends = far_sends[:cut] + first + far_sends[cut:] + second
    near_sends = [(r, 0, width) for r in near]
    wanted = [(0, 0, width)] + far_sends + near_sends
    blocks = pl.pallas_call(
        functools.partial(split_columns, wanted),
        out_shape=[b16((rows_here, count)) for _, _, count in wanted],
        in_specs=[in_vmem],
        out_specs=[in_vmem] * len(wanted),
        compiler_params=PARAMS,
    )(products)
    blocks = dict(zip(wanted, blocks))
    got = {wanted[0]: blocks[wanted[0]]}
    for order, window in ((far_sends, FAR), (near_sends, NEAR)):
        for i, key in enumerate(order):
            block = blocks[key]
            if i >= window:
                block, _ = lax.optimization_barrier((block, got[order[i - window]]))
            got[key] = lax.ppermute(block, "blk", [(k, k ^ key[0]) for k in range(parts)])
    early = [0, *near, *whole]
    gram = pl.pallas_call(
        functools.partial(gram_part, early, rows),
        out_shape=f32((width, width)),
        in_specs=[in_smem] + [in_vmem] * len(early),
        out_specs=in_vmem,
        cost_estimate=pl.CostEstimate(flops=2 * rows * width * width, bytes_accessed=2 * rows * width, transcendentals=0),
        compiler_params=PARAMS,
    )(compat[0], *[got[r, 0, width] for r in early])
    firsts, seconds = [got[key] for key in first], [got[key] for key in second]
    lead_r, lower, lead = pl.pallas_call(
        functools.partial(leading_factor, late, rows),
        out_shape=[f32((h, h))] * 3,
        in_specs=[in_smem, in_smem] + [in_vmem] * (1 + LATE),
        out_specs=[in_vmem] * 3,
        scratch_shapes=[pltpu.VMEM((h, 2 * h), jnp.float32)],
        compiler_params=PARAMS,
    )(compat[0], sizes, gram, *firsts)
    sites = lax.axis_size("seg")

    def onward(x, by):
        return lax.ppermute(x, "seg", [(i, (i + by) % sites) for i in range(sites)])

    lead_in = onward(lead_r, 1)
    factor, rest, trail = pl.pallas_call(
        functools.partial(trailing_factor, late, rows),
        out_shape=(f32((width, width)), f32((h, width)), f32((h, h))),
        in_specs=[in_smem, in_smem] + [in_vmem] * (4 + 2 * LATE),
        out_specs=[in_vmem] * 3,
        scratch_shapes=[pltpu.VMEM((h, 2 * h), jnp.float32)],
        compiler_params=PARAMS,
    )(compat[0], sizes, gram, lead_r, lower, lead, *firsts, *seconds)
    rounds = [(r, 1) for r in early] + [(r, 2) for r in late]
    views = [got[r, 0, width] for r in early] + [x for pair in zip(firsts, seconds) for x in pair]
    ortho = pl.pallas_call(
        functools.partial(orthonormal_rows, rounds, rows),
        out_shape=b16((1, rows, width)),
        in_specs=[in_smem, in_smem] + [in_vmem] * (3 + len(views)),
        out_specs=in_hbm,
        scratch_shapes=[
            pltpu.VMEM((parts, rows_here, width), jnp.bfloat16),
            pltpu.SemaphoreType.DMA((parts,)),
        ],
        compiler_params=PARAMS,
        cost_estimate=pl.CostEstimate(
            flops=4 * rows * width * width, bytes_accessed=4 * rows * width, transcendentals=0
        ),
    )(compat[0], sizes, factor, lead, trail, *views)
    accumulated, by = factor, 1
    while by < sites:
        rest, lead_in = lax.optimization_barrier((rest, lead_in))
        rest_in = onward(rest, by)
        shapes = [f32((width, width)), f32((h, h)), f32((h, width))][: 1 if by * 2 >= sites else 3]
        accumulated, *others = pl.pallas_call(
            functools.partial(chained, by),
            out_shape=shapes,
            in_specs=[in_vmem] * 3,
            out_specs=[in_vmem] * len(shapes),
            compiler_params=PARAMS,
        )(accumulated, lead_in, rest_in)
        by *= 2
        if others:
            lead_in, rest = onward(others[0], by), others[1]
    return (ortho, accumulated[None, None])


def solution(mesh):
    in_specs = (P("seg", "blk", None), P("seg", "blk", None), P("seg", "blk"))
    out_specs = (P("seg", None, "blk"), P("seg", "blk", None, None))
    return jax.shard_map(local, mesh=mesh, in_specs=in_specs, out_specs=out_specs, check_vma=False)
```
